128 devices in a mesh: tile: 32 (over z, y_lo, x), mem: 4 (over y_hi, core).
Axes of the slice: x: 4, y: 4 (y_hi: 2, y_lo: 2; y = y_hi * 2 + y_lo), z: 4, core: 2. Of those that a mesh axis runs over, the one named last changes fastest.
Arguments:
- state: float32 [64, 2, 2048, 512], P('mem', None, 'tile'), may hold values from -10 to 10
- diffusivity: float32 [2048, 512], P('tile'), may hold values from 0.04 to 0.24
- land_sea: int32 [2048, 512], P('tile'), may hold values 0 or 1
- obs_value: float32 [32, 8, 2048], P('tile', 'mem'), may hold values from -8 to 8
- obs_var: float32 [32, 8, 2048], P('tile', 'mem'), may hold values from 16 to 256
- obs_cell: int32 [32, 8, 2048], P('tile', 'mem'), may hold values from 0 to 8191
- obs_count: int32 [32, 8], P('tile', 'mem'), may hold values from 512 to 2048, as said below
Outputs:
- analysis: float32 [64, 2, 2048, 512], P(None, None, 'tile', 'mem')
The draws below stay inside these ranges and needn't reach their ends.
Inputs may be any that keep to these rules, and one draw needn't show every extreme that they name: `obs_count`: slots from a block's count on are empty; some block is full in every draw.
All inputs are finite; a program needn't handle non-finite values. No bound on the sum of `land_sea` on one device may be relied on, other than what follows from the above.
Results may differ from the reference program's by a relative error of at most 0.0003.
Values sent between devices are 32-bit elements; how exact they have to be, the bound alone decides.
No kernel may reach another device: no remote copies, remote signals or barrier semaphores. Data moves between devices by JAX's collectives and lax.ppermute only.
A program may use at most 128 MiB of HBM per device.

```python
import math
import jax
import jax.numpy as jnp
from jax import lax

K = 64
LEV = 2
BS = 64
P_SIZE = 2048
NSI = 4
LOC = 48
NBR = 32
NBC = 8
NX = 2048
NY = 512


def draw_obs_count(key, part):
    key = jax.random.fold_in(key, 7)
    first_key, second_key = jax.random.split(key)
    counts = jax.random.randint(first_key, (NBR * NBC,), P_SIZE // 4, P_SIZE + 1)
    chosen = jax.random.randint(second_key, (), 0, NBR * NBC)
    counts = jnp.where(jnp.arange(NBR * NBC) == chosen, P_SIZE, counts)
    return counts.reshape(NBR, NBC).astype(jnp.int32)


def draw_state(key, part):
    key = jax.random.fold_in(key, 11)
    coeff_key, pattern_key, noise_key = jax.random.split(key, 3)
    pattern_total = 16
    cells = LEV * NX * NY
    patterns = jax.random.normal(pattern_key, (pattern_total, cells), jnp.float32)
    coeffs = jax.random.normal(coeff_key, (K, pattern_total), jnp.float32)
    noise = jax.random.normal(noise_key, (K, cells), jnp.float32)
    decay = 1.2 * 0.7 ** jnp.arange(pattern_total, dtype=jnp.float32)
    shared = jnp.dot(coeffs * decay[None, :], patterns, precision=lax.Precision.HIGHEST, preferred_element_type=jnp.float32)
    field = shared + 0.8 * noise
    return jnp.clip(field, -10.0, 10.0).reshape(K, LEV, NX, NY).astype(jnp.float32)


def touch_ends(array, own_key, low, high):
    spot = [jax.random.randint(jax.random.fold_in(own_key, axis), (), 0, length) for axis, length in enumerate(array.shape)]
    widest = array.shape.index(max(array.shape))
    next_to = spot[:widest] + [(spot[widest] + 1) % array.shape[widest]] + spot[widest + 1:]
    return array.at[tuple(spot)].set(low).at[tuple(next_to)].set(high)


def block_levels(stream_key, extent, cuts, low, largest):
    factor_of = 1.0
    for dim, parts in cuts:
        heights = jax.random.uniform(jax.random.fold_in(jax.random.fold_in(stream_key, 6), dim), (parts,), jnp.float32, low / len(cuts), largest / len(cuts))
        factor_of = factor_of * jnp.repeat(jnp.exp(heights), extent[dim] // parts).reshape((-1,) + (1,) * (len(extent) - 1 - dim))
    return factor_of


def scatter_about(rng, dims, scale, bound, shards=(), kind=jnp.bfloat16):
    values = scale * jax.random.normal(rng, dims, jnp.float32)
    if shards:
        values = values * block_levels(rng, dims, shards, -0.22, 0.18)
    return jnp.clip(values, -bound, bound).astype(kind)


def setup_inputs(seed: int = 0) -> dict:
    seeds = jax.random.split(jax.random.key(seed), 8)
    return {
        "state": draw_state(jax.random.fold_in(seeds[7], 71), 0),
        "diffusivity": jnp.clip(jnp.exp(math.log(0.24) - 1.7917595 * jax.random.uniform(seeds[1], (NX, NY), jnp.float32) ** block_levels(seeds[1], (NX, NY), ((0, 32),), -0.2, 0.2)), 0.04, 0.24),
        "land_sea": touch_ends((jax.random.randint(seeds[2], (NX, NY), 0, 5) < 4).astype(jnp.int32), jax.random.fold_in(seeds[2], 1), 0, 1),
        "obs_value": scatter_about(seeds[3], (NBR, NBC, P_SIZE), 1.5, 8.0, ((0, 32), (1, 4)), jnp.float32),
        "obs_var": jnp.clip(jnp.exp(math.log(256.0) - 2.7725887 * jax.random.uniform(seeds[4], (NBR, NBC, P_SIZE), jnp.float32) ** block_levels(seeds[4], (NBR, NBC, P_SIZE), ((0, 32), (1, 4)), -0.2, 0.2)), 16.0, 256.0),
        "obs_cell": touch_ends(jax.random.randint(seeds[5], (NBR, NBC, P_SIZE), 0, LEV * BS * BS), jax.random.fold_in(seeds[5], 1), 0, (LEV * BS * BS) - 1).astype(jnp.int32),
        "obs_count": draw_obs_count(jax.random.fold_in(seeds[7], 71), 0),
    }


highest_precision = lax.Precision.HIGHEST

def advance(ocean_field, padded, diffuse, seamask):
    laplace = padded[:, :, 2:, 1:-1] + padded[:, :, :-2, 1:-1] + padded[:, :, 1:-1, 2:] + padded[:, :, 1:-1, :-2] - 4.0 * ocean_field
    return ocean_field + seamask * diffuse * laplace

def observe(spread, mean_block, mask_block, obs_cells, values, variance, live_count, block_row, block_col, block_side):
    ens_obs = jnp.take(spread, obs_cells, axis=1)
    innovation = values - jnp.take(mean_block, obs_cells)
    in_block = obs_cells % (block_side * block_side)
    sea_cells = jnp.take(mask_block, in_block)
    live_slots = (jnp.arange(obs_cells.shape[0], dtype=jnp.int32) < live_count).astype(jnp.float32) * sea_cells
    weight = live_slots / variance
    row_pos = (block_row * block_side + in_block // block_side).astype(jnp.float32)
    col_pos = (block_col * block_side + in_block % block_side).astype(jnp.float32)
    obs_info = jnp.stack([weight, innovation, row_pos, col_pos])
    return (ens_obs, obs_info)

def centers(block_row, block_col, block_side):
    center_row = (block_row * block_side).astype(jnp.float32) + 0.5 * (block_side - 1)
    center_col = (block_col * block_side).astype(jnp.float32) + 0.5 * (block_side - 1)
    return (center_row, center_col)

def weighted_gram(ens_obs, obs_info, center_row, center_col, radius):
    off_row = obs_info[2] - center_row
    off_col = obs_info[3] - center_col
    loc_weight = obs_info[0] * jnp.exp(-(off_row * off_row + off_col * off_col) / (2.0 * radius * radius))
    gram_part = jnp.dot(ens_obs * loc_weight, ens_obs.T, precision=highest_precision, preferred_element_type=jnp.float32)
    drive_vec = jnp.dot(ens_obs, loc_weight * obs_info[1], precision=highest_precision, preferred_element_type=jnp.float32)
    return jnp.concatenate([gram_part, drive_vec[None, :]], axis=0)

def analyse(gram_total, own_block, spread, mean_block, mask_block, members, levels, iterations):
    gram_part = gram_total[:members]
    drive_vec = gram_total[members]
    identity = jnp.eye(members, dtype=jnp.float32)
    system = (members - 1.0) * identity + gram_part
    frobenius = jnp.sqrt(jnp.sum(system * system))
    iterate = system / frobenius
    inverse_root = identity
    for repeat in range(iterations):
        correction = 1.5 * identity - 0.5 * jnp.dot(inverse_root, iterate, precision=highest_precision, preferred_element_type=jnp.float32)
        iterate = jnp.dot(iterate, correction, precision=highest_precision, preferred_element_type=jnp.float32)
        inverse_root = jnp.dot(correction, inverse_root, precision=highest_precision, preferred_element_type=jnp.float32)
    root_inv = inverse_root / jnp.sqrt(frobenius)
    inner_vec = jnp.dot(root_inv, drive_vec, precision=highest_precision, preferred_element_type=jnp.float32)
    mean_weight = jnp.dot(root_inv, inner_vec, precision=highest_precision, preferred_element_type=jnp.float32)
    transform = jnp.sqrt(members - 1.0) * root_inv + mean_weight[:, None]
    update = mean_block[None, :] + jnp.dot(transform.T, spread, precision=highest_precision, preferred_element_type=jnp.float32)
    sea_cells = jnp.tile(mask_block, levels)
    return own_block + sea_cells[None, :] * (update - own_block)

def reference(state, diffusivity, land_sea, obs_value, obs_var, obs_cell, obs_count):
    seamask = land_sea.astype(jnp.float32)
    ocean_field = state
    for repeat in range(2):
        padded = jnp.pad(ocean_field, ((0, 0), (0, 0), (1, 1), (1, 1)))
        ocean_field = advance(ocean_field, padded, diffusivity, seamask)
    blocks = ocean_field.reshape(K, LEV, NBR, BS, NBC, BS).transpose(2, 4, 0, 1, 3, 5).reshape(NBR * NBC, K, LEV * BS * BS)
    mask_blocks = seamask.reshape(NBR, BS, NBC, BS).transpose(0, 2, 1, 3).reshape(NBR * NBC, BS * BS)
    values = obs_value.reshape(NBR * NBC, P_SIZE)
    variance = obs_var.reshape(NBR * NBC, P_SIZE)
    obs_cells = obs_cell.reshape(NBR * NBC, P_SIZE)
    counts = obs_count.reshape(NBR * NBC)

    def source(block_index):
        own_block = blocks[block_index]
        mean_block = lax.optimization_barrier(jnp.mean(own_block, axis=0))
        spread = own_block - mean_block[None, :]
        block_row = block_index // NBC
        block_col = block_index % NBC
        ens_obs, obs_info = observe(spread, mean_block, mask_blocks[block_index], obs_cells[block_index], values[block_index], variance[block_index], counts[block_index], block_row, block_col, BS)
        gram_list = []
        for row_step in (-1, 0, 1):
            for col_step in (-1, 0, 1):
                center_row, center_col = centers(block_row + row_step, block_col + col_step, BS)
                gram_list.append(weighted_gram(ens_obs, obs_info, center_row, center_col, LOC))
        return jnp.stack(gram_list)
    indices = jnp.arange(NBR * NBC, dtype=jnp.int32)
    directed = lax.map(source, indices).reshape(NBR, NBC, 9, K + 1, K)
    padded = jnp.pad(directed, ((1, 1), (1, 1), (0, 0), (0, 0), (0, 0)))
    totals = jnp.zeros((NBR, NBC, K + 1, K), jnp.float32)
    for row_step in (-1, 0, 1):
        for col_step in (-1, 0, 1):
            totals = totals + padded[1 + row_step:1 + row_step + NBR, 1 + col_step:1 + col_step + NBC, (1 - row_step) * 3 + (1 - col_step)]
    totals = totals.reshape(NBR * NBC, K + 1, K)

    def target(block_index):
        own_block = blocks[block_index]
        mean_block = lax.optimization_barrier(jnp.mean(own_block, axis=0))
        spread = own_block - mean_block[None, :]
        return analyse(totals[block_index], own_block, spread, mean_block, mask_blocks[block_index], K, LEV, NSI)
    result = lax.map(target, indices)
    return result.reshape(NBR, NBC, K, LEV, BS, BS).transpose(2, 3, 0, 4, 1, 5).reshape(K, LEV, NX, NY)
```

```python
import functools

import jax
import jax.numpy as jnp
from jax import lax
from jax.experimental import pallas as pl
from jax.experimental.pallas import tpu as pltpu
from jax.sharding import PartitionSpec as P

NSI = 4
LOC = 48.0
BS = 64
ML = 16
NI = 48
NE = 16
F32 = jnp.float32
BF16 = jnp.bfloat16
VMEM_LIMIT = 56 * 1024 * 1024
HIGHEST = lax.Precision.HIGHEST


def params(**kw):
    return pltpu.CompilerParams(vmem_limit_bytes=VMEM_LIMIT, **kw)


def lanes():
    return lax.broadcasted_iota(jnp.int32, (8, 128), 1)


def side_sum(x, lane):
    fwd = [pltpu.roll(t, 1, 1) for t in x]
    bwd = [pltpu.roll(t, 127, 1) for t in x]
    zero = jnp.zeros_like(x[0])
    out = []
    for q in range(4):
        left = jnp.where(lane == 0, fwd[q - 1] if q > 0 else zero, fwd[q])
        right = jnp.where(lane == 127, bwd[q + 1] if q < 3 else zero, bwd[q])
        out.append(left + right)
    return out


def step(mid, above, below, md, lane):
    side = side_sum(mid, lane)
    return [
        mid[q] + md[q] * (above[q] + below[q] + side[q] - 4.0 * mid[q]) for q in range(4)
    ]


def pack_store(zs, z0, z1, row, half, lane):
    low = lane < 64
    for q in range(4):
        r0 = pltpu.roll(z0[q], 64, 1)
        r1 = pltpu.roll(z1[q], 64, 1)
        pair = (jnp.where(low, z0[q], r1), jnp.where(low, r0, z1[q]))
        for b in range(2):
            zs[q, b ^ (q & 1), row, pl.ds(8 * half, 8), :] = pair[b]


def fill_md(md, dif, land, rows):
    for r8 in sorted({r // 8 for r in rows}):
        m = land[8 * r8 : 8 * r8 + 8, :].astype(F32) * dif[8 * r8 : 8 * r8 + 8, :]
        for j in range(8):
            for q in range(4):
                md[8 * r8 + j, q] = jnp.broadcast_to(
                    m[j : j + 1, 128 * q : 128 * q + 128], (8, 128)
                )


def md_row(md, r):
    return [md[r, q] for q in range(4)]


def send_out(zs, outs, me, sems):
    copies = []
    for k in range(2):
        copies.append(pltpu.make_async_copy(zs.at[me ^ k], outs[k], sems.at[k]))
    for k in range(2, 4):
        for fs in range(2):
            n = 2 * k - 2 + fs
            copies.append(pltpu.make_async_copy(zs.at[me ^ k, fs], outs[n], sems.at[n]))
    for c in copies:
        c.start()
    for c in copies:
        c.wait()


def interior_kernel(state, dif, land, o0, o1, o2f, o2s, o3f, o3s, hup, hdn, xs, zs, md, isem, osem):
    me = lax.axis_index("mem")
    copies = [
        [
            pltpu.make_async_copy(
                state.at[pl.ds(8 * h, 8), :, :, pl.ds(128 * q, 128)],
                xs.at[q, pl.ds(8 * h, 8)],
                isem.at[h, q],
            )
            for q in range(4)
        ]
        for h in range(2)
    ]
    for h in range(2):
        for c in copies[h]:
            c.start()
    fill_md(md, dif, land, range(64))
    lane = lanes()
    xf = xs.reshape(4 * ML * 2 * 64, 128)

    def load(h, lev, r):
        return [xf[pl.ds(((q * ML + 8 * h) * 2 + lev) * 64 + r, 8, stride=128), :] for q in range(4)]

    for h in range(2):
        for c in copies[h]:
            c.wait()
        for lev in range(2):
            for j in range(2):
                top = load(h, lev, j)
                bot = load(h, lev, 62 + j)
                for q in range(4):
                    at = (pl.ds(j * 32 + lev * 16 + 8 * h, 8), pl.ds(128 * q, 128))
                    hdn[at] = top[q]
                    hup[at] = bot[q]

        def first(r):
            m = md_row(md, r)
            out = []
            for lev in range(2):
                out.append(step(load(h, lev, r), load(h, lev, r - 1), load(h, lev, r + 1), m, lane))
            return out

        def body(r, carry):
            xa, xm, ya, ym = carry
            m1 = md_row(md, r)
            m0 = md_row(md, r - 1)
            xb = [load(h, lev, r + 1) for lev in range(2)]
            yb = [step(xm[lev], xa[lev], xb[lev], m1, lane) for lev in range(2)]
            z = [step(ym[lev], ya[lev], yb[lev], m0, lane) for lev in range(2)]
            pack_store(zs, z[0], z[1], r - 9, h, lane)
            return xm, xb, ym, yb

        start = (
            [load(h, lev, 8) for lev in range(2)],
            [load(h, lev, 9) for lev in range(2)],
            first(7),
            first(8),
        )
        lax.fori_loop(9, 57, body, start)
    for h_out, r in ((hup, 63), (hdn, 0)):
        for q in range(4):
            h_out[64:72, 128 * q : 128 * q + 128] = md[r, q]
    send_out(zs, (o0, o1, o2f, o2s, o3f, o3s), me, osem)


def edge_kernel(state, dif, land, above, below, o0, o1, o2f, o2s, o3f, o3s, xs, zs, md, isem, osem):
    me = lax.axis_index("mem")
    copies = [
        pltpu.make_async_copy(
            state.at[:, :, pl.ds(48 * s, 16), pl.ds(128 * q, 128)], xs.at[s, q], isem.at[s, q]
        )
        for s in range(2)
        for q in range(4)
    ]
    for c in copies:
        c.start()
    fill_md(md, dif, land, [*range(16), *range(48, 64)])
    lane = lanes()
    xf = xs.reshape(2 * 4 * ML * 2 * 16, 128)
    for c in copies:
        c.wait()

    def load(h, lev, r):
        if r < 0 or r > 63:
            ref, j = (above, r + 2) if r < 0 else (below, r - 64)
            return [
                ref[pl.ds(j * 32 + lev * 16 + 8 * h, 8), pl.ds(128 * q, 128)] for q in range(4)
            ]
        s, rr = (0, r) if r < 16 else (1, r - 48)
        return [
            xf[pl.ds((((s * 4 + q) * ML + 8 * h) * 2 + lev) * 16 + rr, 8, stride=32), :]
            for q in range(4)
        ]

    def mdrow(r):
        if r < 0:
            return [above[64:72, 128 * q : 128 * q + 128] for q in range(4)]
        if r > 63:
            return [below[64:72, 128 * q : 128 * q + 128] for q in range(4)]
        return md_row(md, r)

    for side in range(2):
        base = 56 * side
        for h in range(2):
            x = {}
            y = {}
            for r in range(base - 2, base + 10):
                x[r] = [load(h, lev, r) for lev in range(2)]
                if r >= base:
                    m = mdrow(r - 1)
                    y[r - 1] = [
                        step(x[r - 1][lev], x[r - 2][lev], x[r][lev], m, lane) for lev in range(2)
                    ]
                if r >= base + 2:
                    m = mdrow(r - 2)
                    z = [
                        step(y[r - 2][lev], y[r - 3][lev], y[r - 1][lev], m, lane)
                        for lev in range(2)
                    ]
                    pack_store(zs, z[0], z[1], r - 2 - base + 8 * side, h, lane)
    send_out(zs, (o0, o1, o2f, o2s, o3f, o3s), me, osem)


def split_shapes(n):
    pair = jax.ShapeDtypeStruct((2, n, ML, 128), F32)
    one = jax.ShapeDtypeStruct((n, ML, 128), F32)
    return [pair, pair, one, one, one, one]


ANY = pl.BlockSpec(memory_space=pl.ANY)
VM = pl.BlockSpec(memory_space=pltpu.VMEM)


def forecast_interior(state, dif, land):
    halo = jax.ShapeDtypeStruct((72, 512), F32)
    return pl.pallas_call(
        interior_kernel,
        out_shape=split_shapes(NI) + [halo, halo],
        in_specs=[ANY, VM, VM],
        out_specs=[ANY] * 6 + [VM, VM],
        scratch_shapes=[
            pltpu.VMEM((4, ML, 2, 64, 128), F32),
            pltpu.VMEM((4, 2, NI, ML, 128), F32),
            pltpu.VMEM((64, 4, 8, 128), F32),
            pltpu.SemaphoreType.DMA((2, 4)),
            pltpu.SemaphoreType.DMA((6,)),
        ],
        compiler_params=params(),
        cost_estimate=pl.CostEstimate(flops=40_000_000, bytes_accessed=8_000_000, transcendentals=0),
        name="forecast_interior",
    )(state, dif, land)


def forecast_edge(state, dif, land, above, below):
    return pl.pallas_call(
        edge_kernel,
        out_shape=split_shapes(NE),
        in_specs=[ANY, VM, VM, VM, VM],
        out_specs=[ANY] * 6,
        scratch_shapes=[
            pltpu.VMEM((2, 4, ML, 2, 16, 128), F32),
            pltpu.VMEM((4, 2, NE, ML, 128), F32),
            pltpu.VMEM((64, 4, 8, 128), F32),
            pltpu.SemaphoreType.DMA((2, 4)),
            pltpu.SemaphoreType.DMA((6,)),
        ],
        compiler_params=params(),
        cost_estimate=pl.CostEstimate(flops=14_000_000, bytes_accessed=3_000_000, transcendentals=0),
        name="forecast_edge",
    )(state, dif, land, above, below)


def two_terms(x):
    hi = x.astype(BF16)
    lo = (x - hi.astype(F32)).astype(BF16)
    return hi, lo


def dot_nt(a, b):
    return lax.dot_general(a, b, (((1,), (1,)), ((), ())), preferred_element_type=F32)


def weight_kernel(count, cell, value, var, land, out, sea_out):
    me = lax.axis_index("mem")
    odd = me & 1
    slots = cell.shape[2]
    rows64 = lax.broadcasted_iota(jnp.int32, (64, slots), 0)
    rows128 = lax.broadcasted_iota(jnp.int32, (128, slots), 0)
    slot = lax.broadcasted_iota(jnp.int32, (1, slots), 1)
    sea = land[:, pl.ds(pl.multiple_of(me * 128, 128), 128)].astype(F32)
    lane = lax.broadcasted_iota(jnp.int32, (64, 128), 1)
    turned = pltpu.roll(sea, 64, 1)
    seas = (jnp.where(lane < 64, sea, turned), jnp.where(lane < 64, turned, sea))
    for b in range(2):
        c = cell[0, b : b + 1, :]
        live = slot < count[0, b]
        w = jnp.where(live, 1.0 / var[0, b : b + 1, :], 0.0)
        u = w * value[0, b : b + 1, :]
        at_row = rows64 == ((c >> 6) & 63)
        at_lane = rows128 == (((c >> 12) << 6) | (c & 63))
        terms = []
        for v in (w, u):
            t0 = v.astype(BF16).astype(F32)
            r1 = v - t0
            t1 = r1.astype(BF16).astype(F32)
            t2 = r1 - t1
            terms += [jnp.where(at_row, t, 0.0).astype(BF16) for t in (t0, t1, t2)]
        lhs = jnp.concatenate(terms, axis=0)
        rhs = jnp.where(at_lane, 1.0, 0.0).astype(BF16)
        full = dot_nt(lhs, rhs)
        fs = b ^ odd
        out[fs, 0] = (full[0:64] + full[64:128] + full[128:192]) * seas[b]
        out[fs, 1] = (full[192:256] + full[256:320] + full[320:384]) * seas[b]
        sea_out[fs] = seas[b]


def cell_weights(count, cell, value, var, land):
    return pl.pallas_call(
        weight_kernel,
        out_shape=[
            jax.ShapeDtypeStruct((2, 2, 64, 128), F32),
            jax.ShapeDtypeStruct((2, 64, 128), F32),
        ],
        in_specs=[pl.BlockSpec(memory_space=pltpu.SMEM), VM, VM, VM, VM],
        out_specs=[VM, VM],
        compiler_params=params(),
        cost_estimate=pl.CostEstimate(flops=8_000_000, bytes_accessed=1_000_000, transcendentals=0),
        name="cell_weights",
    )(count, cell, value, var, land)


def gauss(off):
    return jnp.exp(-(off * off) / (2.0 * LOC * LOC))


def gram_group(pieces, xo, wu, row0, acc, lh, ll, rh, rl, me):
    for k in range(4):
        at = pl.multiple_of((me ^ k) * ML, ML)
        xo[:, pl.ds(at, ML), :] = pieces[k][...]
    sub = lax.broadcasted_iota(jnp.int32, (8, 128), 0)
    r = (sub + row0).astype(F32)
    w = wu[0, 0]
    u = wu[0, 1]
    c = (lax.broadcasted_iota(jnp.int32, (1, 128), 1) & 63).astype(F32)
    er = [gauss(r - 31.5 - 64.0 * i) for i in (-1, 0, 1)]
    ec = [gauss(c - 31.5 - 64.0 * j) for j in (-1, 0, 1)]
    wi = [w * e for e in er]
    ui = [u * e for e in er]
    sub16 = lax.broadcasted_iota(jnp.int32, (16, 128), 0)
    for rr in range(8):
        x = xo[rr]
        mean = jnp.sum(x, axis=0, keepdims=True) * (1.0 / 64.0)
        s = x - mean
        cols = pl.ds(128 * rr, 128)
        for i in range(3):
            wrow = wi[i][rr : rr + 1]
            hi, lo = two_terms(s * wrow)
            lh[pl.ds(80 * i, 64), cols] = hi
            ll[pl.ds(80 * i, 64), cols] = lo
            drive = ui[i][rr : rr + 1] - wrow * mean
            hi, lo = two_terms(jnp.where(sub16 == 0, drive, 0.0))
            lh[pl.ds(80 * i + 64, 16), cols] = hi
            ll[pl.ds(80 * i + 64, 16), cols] = lo
        for j in range(3):
            hi, lo = two_terms(s * ec[j])
            rh[pl.ds(64 * j, 64), cols] = hi
            rl[pl.ds(64 * j, 64), cols] = lo
    a = lh[...]
    b = rh[...]
    acc[...] += dot_nt(a, b) + dot_nt(a, rl[...]) + dot_nt(ll[...], b)


GRAM_SCRATCH = [
    pltpu.VMEM((240, 1024), BF16),
    pltpu.VMEM((240, 1024), BF16),
    pltpu.VMEM((192, 1024), BF16),
    pltpu.VMEM((192, 1024), BF16),
]


def first_kernel(i0, i1, i2, i3, e0, e1, e2, e3, wu, acc, xi, xe, msg, *tmp):
    me = lax.axis_index("mem")
    g = pl.program_id(0)

    @pl.when(g == 0)
    def _():
        acc[...] = jnp.zeros_like(acc)

    @pl.when(g < 6)
    def _():
        gram_group((i0.at[0], i1.at[0], i2, i3), xi, wu, 8 * g + 8, acc, *tmp, me)

    @pl.when(g >= 6)
    def _():
        gram_group((e0.at[0], e1.at[0], e2, e3), xe, wu, 56 * (g - 6), acc, *tmp, me)

    @pl.when(g == 7)
    def _():
        d = acc[...]
        msg[...] = jnp.where((me & 1) == 1, d[:, 128:192], d[:, 0:64])


def second_kernel(i0, i1, i2, i3, wu, acc, xi, *tmp):
    me = lax.axis_index("mem")
    g = pl.program_id(0)

    @pl.when(g == 0)
    def _():
        acc[...] = jnp.zeros_like(acc)

    gram_group((i0.at[0], i1.at[0], i2, i3), xi, wu, 8 * g + 8, acc, *tmp, me)


def third_kernel(e0, e1, e2, e3, wu, df, ds, mid, xe, msg, acc, *tmp):
    me = lax.axis_index("mem")
    g = pl.program_id(0)

    @pl.when(g == 0)
    def _():
        acc[...] = ds[...]

    gram_group((e0.at[0], e1.at[0], e2, e3), xe, wu, 56 * g, acc, *tmp, me)

    @pl.when(g == 1)
    def _():
        odd = (me & 1) == 1
        f = df[...]
        s = acc[...]
        b0 = jnp.where(odd, s, f)
        b1 = jnp.where(odd, f, s)
        mid[...] = jnp.concatenate(
            [b0[:, 64:128] + b1[:, 0:64], b0[:, 128:192] + b1[:, 64:128]], axis=1
        )
        msg[...] = jnp.where(odd, b0[:, 0:64], b1[:, 128:192])


def piece_specs(fs, index):
    pair = pl.BlockSpec((1, 8, ML, 128), lambda g: (fs, index(g), 0, 0))
    one = pl.BlockSpec((8, ML, 128), lambda g: (index(g), 0, 0))
    return [pair, pair, one, one]


def gram_shapes():
    return jax.ShapeDtypeStruct((240, 192), F32), jax.ShapeDtypeStruct((240, 64), F32)


WHOLE = lambda shape: pl.BlockSpec(shape, lambda g: (0,) * len(shape))


def gram_cost(groups):
    return pl.CostEstimate(
        flops=groups * 3 * 2 * 240 * 192 * 1024, bytes_accessed=groups * 600_000, transcendentals=0
    )


def gram_first(inner, edge, wu):
    acc, msg = gram_shapes()
    ii = lambda g: jnp.minimum(g, 5)
    ei = lambda g: jnp.maximum(g - 6, 0)
    wi = lambda g: jnp.where(g < 6, g + 1, jnp.where(g == 6, 0, 7))
    return pl.pallas_call(
        first_kernel,
        grid=(8,),
        out_shape=[
            acc,
            jax.ShapeDtypeStruct((NI, 64, 128), F32),
            jax.ShapeDtypeStruct((NE, 64, 128), F32),
            msg,
        ],
        in_specs=piece_specs(0, ii)
        + piece_specs(0, ei)
        + [pl.BlockSpec((1, 2, 8, 128), lambda g: (0, 0, wi(g), 0))],
        out_specs=[
            WHOLE((240, 192)),
            pl.BlockSpec((8, 64, 128), lambda g: (ii(g), 0, 0)),
            pl.BlockSpec((8, 64, 128), lambda g: (ei(g), 0, 0)),
            WHOLE((240, 64)),
        ],
        scratch_shapes=GRAM_SCRATCH,
        compiler_params=params(),
        cost_estimate=gram_cost(8),
        name="gram_first",
    )(*inner, *edge, wu)


def gram_second(inner, wu):
    acc, _ = gram_shapes()
    ii = lambda g: g
    return pl.pallas_call(
        second_kernel,
        grid=(6,),
        out_shape=[acc, jax.ShapeDtypeStruct((NI, 64, 128), F32)],
        in_specs=piece_specs(1, ii) + [pl.BlockSpec((1, 2, 8, 128), lambda g: (1, 0, g + 1, 0))],
        out_specs=[WHOLE((240, 192)), pl.BlockSpec((8, 64, 128), lambda g: (g, 0, 0))],
        scratch_shapes=GRAM_SCRATCH,
        compiler_params=params(),
        cost_estimate=gram_cost(6),
        name="gram_second",
    )(*inner, wu)


def gram_third(edge, wu, df, ds):
    _, msg = gram_shapes()
    ei = lambda g: g
    return pl.pallas_call(
        third_kernel,
        grid=(2,),
        out_shape=[
            jax.ShapeDtypeStruct((240, 128), F32),
            jax.ShapeDtypeStruct((NE, 64, 128), F32),
            msg,
        ],
        in_specs=piece_specs(1, ei)
        + [
            pl.BlockSpec((1, 2, 8, 128), lambda g: (1, 0, 7 * g, 0)),
            WHOLE((240, 192)),
            WHOLE((240, 192)),
        ],
        out_specs=[
            WHOLE((240, 128)),
            pl.BlockSpec((8, 64, 128), lambda g: (g, 0, 0)),
            WHOLE((240, 64)),
        ],
        scratch_shapes=[pltpu.VMEM((240, 192), F32)] + GRAM_SCRATCH,
        compiler_params=params(),
        cost_estimate=gram_cost(2),
        name="gram_third",
    )(*edge, wu, df, ds)


def join_kernel(mid, core, border, down, own, up):
    odd = (lax.axis_index("mem") & 1) == 1
    c = core[...]
    b = border[...]
    q = mid[...] + jnp.concatenate([jnp.where(odd, c, b), jnp.where(odd, b, c)], axis=1)
    down[...] = q[0:80]
    own[...] = q[80:160]
    up[...] = q[160:240]


def join(mid, core, border):
    one = jax.ShapeDtypeStruct((80, 128), F32)
    return pl.pallas_call(
        join_kernel,
        out_shape=[one, one, one],
        in_specs=[VM, VM, VM],
        out_specs=[VM, VM, VM],
        compiler_params=params(),
        name="join_grams",
    )(mid, core, border)


def dot32(a, b):
    return lax.dot_general(
        a, b, (((1,), (0,)), ((), ())), precision=HIGHEST, preferred_element_type=F32
    )


def weights_of(gram, drive):
    n = gram.shape[0]
    eye = (
        lax.broadcasted_iota(jnp.int32, (n, n), 0) == lax.broadcasted_iota(jnp.int32, (n, n), 1)
    ).astype(F32)
    system = (n - 1.0) * eye + gram
    squares = jnp.sum(jnp.sum(system * system, axis=1, keepdims=True), axis=0, keepdims=True)
    frob = jnp.sqrt(squares)
    iterate = system / frob
    root = None
    for it in range(NSI):
        prod = iterate if root is None else dot32(root, iterate)
        corr = 1.5 * eye - 0.5 * prod
        if it < NSI - 1:
            iterate = dot32(iterate, corr)
        root = corr if root is None else dot32(corr, root)
    half = root / jnp.sqrt(frob)
    row = dot32(dot32(jnp.broadcast_to(drive, (8, n)), half), half)
    return jnp.sqrt(n - 1.0) * half + row[0:1]


def analysis_kernel(own, fromlow, fromhigh, xfi, xfe, xsi, xse, sea, out, tt, rhs, ys):
    me = lax.axis_index("mem")
    odd = (me & 1) == 1
    g = pl.program_id(0)

    @pl.when(g == 0)
    def _():
        tot = own[...] + fromlow[...] + fromhigh[...]
        t0 = tot[:, 0:64]
        t1 = tot[:, 64:128]
        for fs, t in enumerate((jnp.where(odd, t1, t0), jnp.where(odd, t0, t1))):
            hi, lo = two_terms(weights_of(t[0:64], t[64:65]))
            tt[fs] = jnp.concatenate([hi, hi, lo], axis=1)

    lane = lax.broadcasted_iota(jnp.int32, (64, 128), 1)

    def rows(refs):
        for fs in range(2):
            for rr in range(8):
                x = refs[fs][rr]
                mean = jnp.sum(x, axis=0, keepdims=True) * (1.0 / 64.0)
                hi, lo = two_terms(x - mean)
                cols = pl.ds(128 * rr, 128)
                rhs[fs, 0:64, cols] = hi
                rhs[fs, 64:128, cols] = lo
                rhs[fs, 128:192, cols] = hi
        upd = [
            lax.dot_general(
                tt[fs], rhs[fs], (((1,), (0,)), ((), ())), preferred_element_type=F32
            )
            for fs in range(2)
        ]
        for rr in range(8):
            res = []
            for fs in range(2):
                x = refs[fs][rr]
                mean = jnp.sum(x, axis=0, keepdims=True) * (1.0 / 64.0)
                up = mean + upd[fs][:, 128 * rr : 128 * rr + 128]
                res.append(x + sea[fs, rr : rr + 1, :] * (up - x))
            b0 = jnp.where(odd, res[1], res[0])
            b1 = jnp.where(odd, res[0], res[1])
            ys[0, pl.ds(64 * rr, 64), :] = jnp.where(lane < 64, b0, pltpu.roll(b1, 64, 1))
            ys[1, pl.ds(64 * rr, 64), :] = jnp.where(lane < 64, pltpu.roll(b0, 64, 1), b1)
        for m in range(64):
            for lev in range(2):
                out[m, lev] = ys[lev, pl.ds(m, 8, stride=64), :]

    edge = jnp.logical_or(g == 0, g == 7)

    @pl.when(edge)
    def _():
        rows((xfe, xse))

    @pl.when(jnp.logical_not(edge))
    def _():
        rows((xfi, xsi))


def analysis(own, fromlow, fromhigh, xfi, xfe, xsi, xse, sea):
    ii = lambda g: (jnp.clip(g - 1, 0, 5), 0, 0)
    ei = lambda g: (jnp.where(g == 7, 1, 0), 0, 0)
    inner = pl.BlockSpec((8, 64, 128), ii)
    edge = pl.BlockSpec((8, 64, 128), ei)
    return pl.pallas_call(
        analysis_kernel,
        grid=(8,),
        out_shape=jax.ShapeDtypeStruct((64, 2, 64, 128), F32),
        in_specs=[WHOLE((80, 128))] * 3
        + [inner, edge, inner, edge]
        + [pl.BlockSpec((2, 8, 128), lambda g: (0, g, 0))],
        out_specs=pl.BlockSpec((64, 2, 8, 128), lambda g: (0, 0, g, 0)),
        scratch_shapes=[
            pltpu.VMEM((2, 64, 192), BF16),
            pltpu.VMEM((2, 192, 1024), BF16),
            pltpu.VMEM((2, 512, 128), F32),
        ],
        compiler_params=params(),
        name="analysis",
    )(own, fromlow, fromhigh, xfi, xfe, xsi, xse, sea)


def per_device(state, diffusivity, land_sea, obs_value, obs_var, obs_cell, obs_count):
    tiles = lax.axis_size("tile")
    up = [(i, i + 1) for i in range(tiles - 1)]
    down = [(i + 1, i) for i in range(tiles - 1)]
    swap = lambda k: [(i, i ^ k) for i in range(4)]

    a = forecast_interior(state, diffusivity, land_sea)
    a2f = lax.ppermute(a[2], "mem", swap(2))
    a3f = lax.ppermute(a[4], "mem", swap(3))
    above = lax.ppermute(a[6], "tile", up)
    below = lax.ppermute(a[7], "tile", down)
    a1 = lax.ppermute(a[1], "mem", swap(1))
    wu, sea = cell_weights(obs_count, obs_cell, obs_value, obs_var, land_sea)
    e = forecast_edge(state, diffusivity, land_sea, above, below)
    e2f = lax.ppermute(e[2], "mem", swap(2))
    e3f = lax.ppermute(e[4], "mem", swap(3))
    e1 = lax.ppermute(e[1], "mem", swap(1))
    a2s = lax.ppermute(a[3], "mem", swap(2))
    a3s = lax.ppermute(a[5], "mem", swap(3))
    e2s = lax.ppermute(e[3], "mem", swap(2))
    e3s = lax.ppermute(e[5], "mem", swap(3))
    df, xfi, xfe, border = gram_first((a[0], a1, a2f, a3f), (e[0], e1, e2f, e3f), wu)
    border = lax.ppermute(border, "mem", [(1, 2), (2, 1)])
    ds, xsi = gram_second((a[0], a1, a2s, a3s), wu)
    mid, xse, core = gram_third((e[0], e1, e2s, e3s), wu, df, ds)
    core = lax.ppermute(core, "mem", swap(1))
    to_low, own, to_high = join(mid, core, border)
    fromlow = lax.ppermute(to_high, "tile", up)
    fromhigh = lax.ppermute(to_low, "tile", down)
    return analysis(own, fromlow, fromhigh, xfi, xfe, xsi, xse, sea)


def solution(mesh):
    return jax.shard_map(
        per_device,
        mesh=mesh,
        in_specs=(
            P("mem", None, "tile", None),
            P("tile", None),
            P("tile", None),
            P("tile", "mem", None),
            P("tile", "mem", None),
            P("tile", "mem", None),
            P("tile", "mem"),
        ),
        out_specs=P(None, None, "tile", "mem"),
        check_vma=False,
    )
```

```python
import functools

import jax
import jax.numpy as jnp
from jax import lax
from jax.experimental import pallas as pl
from jax.experimental.pallas import tpu as pltpu
from jax.sharding import PartitionSpec as P

NSI = 4
LOC = 48.0
BS = 64
UNROLL = 4
UNROLL_B = 6
ML = 16
NE = 16
F32 = jnp.float32
BF16 = jnp.bfloat16
VMEM_LIMIT = 56 * 1024 * 1024
HIGHEST = lax.Precision.HIGHEST


def params(**kw):
    return pltpu.CompilerParams(vmem_limit_bytes=VMEM_LIMIT, **kw)


def two_terms(x):
    hi = x.astype(BF16)
    lo = (x - hi.astype(F32)).astype(BF16)
    return hi, lo


def pack_store(zs, z, row, lane):
    low = lane < 64
    for q in range(4):
        r0 = pltpu.roll(z[0][q], 64, 1)
        r1 = pltpu.roll(z[1][q], 64, 1)
        pair = (jnp.where(low, z[0][q], r1), jnp.where(low, r0, z[1][q]))
        for b in range(2):
            zs[q, b ^ (q & 1), row] = pair[b]


def fill_md(md, dif, land, rows):
    for r8 in sorted({r // 8 for r in rows}):
        m = land[8 * r8 : 8 * r8 + 8, :].astype(F32) * dif[8 * r8 : 8 * r8 + 8, :]
        for j in range(8):
            if 8 * r8 + j in rows:
                for q in range(4):
                    md[8 * r8 + j, q] = jnp.broadcast_to(
                        m[j : j + 1, 128 * q : 128 * q + 128], (8, 128)
                    )


def md_row(md, r):
    return [jnp.concatenate([md[r, q], md[r, q]], axis=0) for q in range(4)]


class Rows:
    def __init__(self, state, xs, sems, segments):
        self.n = sum(length for _, length in segments)
        self.stride = 2 * self.n + 8
        self.flat = xs.reshape(4 * ML * self.stride, 128)
        self.segments = segments
        self.copies = []
        for lev in range(2):
            todo = []
            at = 0
            for i, (start, length) in enumerate(segments):
                for q in range(4):
                    todo.append(
                        pltpu.make_async_copy(
                            state.at[:, lev, pl.ds(start, length), pl.ds(128 * q, 128)],
                            xs.at[q, :, pl.ds(lev * self.n + at, length)],
                            sems.at[lev, i * 4 + q],
                        )
                    )
                at += length
            self.copies.append(todo)

    def start(self):
        for todo in self.copies:
            for c in todo:
                c.start()

    def wait(self, lev):
        for c in self.copies[lev]:
            c.wait()

    def offset(self, r):
        at = 0
        for start, length in self.segments:
            if start <= r < start + length:
                return r - start + at
            at += length
        raise ValueError(r)

    def load(self, lev, off):
        return [
            self.flat[pl.ds(q * ML * self.stride + lev * self.n + off, ML, stride=self.stride), :]
            for q in range(4)
        ]


class Stencil:
    def __init__(self, x, y):
        self.x = x
        self.y = y
        self.lane = lax.broadcasted_iota(jnp.int32, (ML, 128), 1)

    def put(self, ref, p, lev, tiles):
        for q in range(4):
            ref[p, lev, :, pl.ds(128 * q, 128)] = tiles[q]

    def step(self, ref, p, lev, md):
        mid = [ref[p, lev, :, pl.ds(128 * q, 128)] for q in range(4)]
        fwd = [pltpu.roll(t, 1, 1) for t in mid]
        bwd = [pltpu.roll(t, 127, 1) for t in mid]
        zero = jnp.zeros_like(mid[0])
        out = []
        for q in range(4):
            cols = pl.ds(128 * q, 128)
            left = jnp.where(self.lane == 0, fwd[q - 1] if q > 0 else zero, fwd[q])
            right = jnp.where(self.lane == 127, bwd[q + 1] if q < 3 else zero, bwd[q])
            near = (ref[p - 1, lev, :, cols] + ref[p + 1, lev, :, cols]) + (left + right)
            out.append(mid[q] + md[q] * (near - 4.0 * mid[q]))
        return out


class Sender:
    def __init__(self, zs, outs, me, sems):
        self.zs = zs
        self.outs = outs
        self.me = me
        self.sems = sems
        self.copies = []

    def send(self, at, length):
        for k in range(4):
            c = pltpu.make_async_copy(
                self.zs.at[self.me ^ k, :, pl.ds(at, length)],
                self.outs[k].at[:, pl.ds(at, length)],
                self.sems.at[len(self.copies)],
            )
            c.start()
            self.copies.append(c)

    def wait(self):
        for c in self.copies:
            c.wait()


SEG_A = ((0, 32), (56, 8))
SEG_B = ((16, 48),)
SEG_C = ((0, 16), (48, 16))
ROWS_A = (8, 16)
ROWS_B = (24, 32)


def plain_rows(rows, st, md, zs, sender, r0, n):
    off = rows.offset(r0 - 2)
    lane = lax.broadcasted_iota(jnp.int32, (ML, 128), 1)
    for lev in range(2):
        rows.wait(lev)

        @pl.loop(0, n + 4, unroll=2)
        def _(p, lev=lev):
            st.put(st.x, p, lev, rows.load(lev, off + p))

    @pl.loop(1, n + 3, unroll=UNROLL_B)
    def _(p):
        m = md_row(md, p + (r0 - 2))
        for lev in range(2):
            st.put(st.y, p, lev, st.step(st.x, p, lev, m))

    for blk in range(n // 8):

        @pl.loop(8 * blk, 8 * blk + 8, unroll=UNROLL)
        def _(i):
            m = md_row(md, i + r0)
            pack_store(zs, [st.step(st.y, i + 2, lev, m) for lev in range(2)], i, lane)

        sender.send(8 * blk, 8)
    sender.wait()


def first_rows_kernel(
    state, dif, land, o0, o1, o2, o3, hup, hdn, xs, zs, md, x, y, isem, osem
):
    rows = Rows(state, xs, isem, SEG_A)
    rows.start()
    r0, n = ROWS_A
    fill_md(md, dif, land, [0, 63, *range(r0 - 1, r0 + n + 1)])
    st = Stencil(x, y)
    sender = Sender(zs, (o0, o1, o2, o3), lax.axis_index("mem"), osem)
    plain_rows(rows, st, md, zs, sender, r0, n)
    for j in range(2):
        for lev in range(2):
            for ref, r in ((hdn, j), (hup, 62 + j)):
                v = rows.load(lev, rows.offset(r))
                for q in range(4):
                    ref[pl.ds(j * 32 + lev * 16, 16), pl.ds(128 * q, 128)] = v[q]
    for ref, r in ((hup, 63), (hdn, 0)):
        for q in range(4):
            ref[64:72, 128 * q : 128 * q + 128] = md[r, q]


def inner_rows_kernel(
    state, dif, land, o0, o1, o2, o3, xs, zs, md, x, y, isem, osem
):
    rows = Rows(state, xs, isem, SEG_B)
    rows.start()
    r0, n = ROWS_B
    fill_md(md, dif, land, range(r0 - 1, r0 + n + 1))
    st = Stencil(x, y)
    sender = Sender(zs, (o0, o1, o2, o3), lax.axis_index("mem"), osem)
    plain_rows(rows, st, md, zs, sender, r0, n)


def edge_rows_kernel(
    state, dif, land, above, below, o0, o1, o2, o3, xs, zs, md, x, y, isem, osem
):
    rows = Rows(state, xs, isem, SEG_C)
    rows.start()
    fill_md(md, dif, land, [*range(9), *range(55, 64)])
    st = Stencil(x, y)
    sender = Sender(zs, (o0, o1, o2, o3), lax.axis_index("mem"), osem)
    lane = lax.broadcasted_iota(jnp.int32, (ML, 128), 1)
    for ref, p0 in ((above, 0), (below, 22)):
        for j in range(2):
            for lev in range(2):
                at = pl.ds(j * 32 + lev * 16, 16)
                st.put(x, p0 + j, lev, [ref[at, 128 * q : 128 * q + 128] for q in range(4)])
    for lev in range(2):
        rows.wait(lev)

        @pl.loop(0, 10, unroll=2)
        def _(i, lev=lev):
            st.put(x, i + 2, lev, rows.load(lev, i))
            st.put(x, i + 12, lev, rows.load(lev, i + 22))

    def outside(ref):
        tiles = [ref[64:72, 128 * q : 128 * q + 128] for q in range(4)]
        return [jnp.concatenate([t, t], axis=0) for t in tiles]

    for p, ref in ((1, above), (22, below)):
        for lev in range(2):
            st.put(y, p, lev, st.step(x, p, lev, outside(ref)))

    @pl.loop(0, 9, unroll=3)
    def _(i):
        m = md_row(md, i)
        w = md_row(md, i + 55)
        for lev in range(2):
            st.put(y, i + 2, lev, st.step(x, i + 2, lev, m))
            st.put(y, i + 13, lev, st.step(x, i + 13, lev, w))

    for blk in range(2):

        @pl.loop(0, 8, unroll=UNROLL)
        def _(i, blk=blk):
            m = md_row(md, i + 56 * blk)
            z = [st.step(y, i + 2 + 12 * blk, lev, m) for lev in range(2)]
            pack_store(zs, z, i + 8 * blk, lane)

        sender.send(8 * blk, 8)
    sender.wait()


ANY = pl.BlockSpec(memory_space=pl.ANY)
VM = pl.BlockSpec(memory_space=pltpu.VMEM)


def us(t):
    return pl.CostEstimate(
        flops=int(t * 1.1e9), bytes_accessed=int(t * 3.4e6), transcendentals=0
    )


def piece(n):
    return jax.ShapeDtypeStruct((2, n, ML, 128), F32)


def forecast_call(kernel, name, segments, n, count, outs, extra_out, args, cost):
    loaded = sum(length for _, length in segments)
    kept = (count, 2, ML, 512)
    return pl.pallas_call(
        kernel,
        out_shape=outs + extra_out,
        in_specs=[ANY] + [VM] * (len(args) - 1),
        out_specs=[ANY] * len(outs) + [VM] * len(extra_out),
        scratch_shapes=[
            pltpu.VMEM((4, ML, 2 * loaded + 8, 128), F32),
            pltpu.VMEM((4, 2, n, ML, 128), F32),
            pltpu.VMEM((64, 4, 8, 128), F32),
            pltpu.VMEM(kept, F32),
            pltpu.VMEM(kept, F32),
            pltpu.SemaphoreType.DMA((2, 4 * len(segments))),
            pltpu.SemaphoreType.DMA((n // 8 * len(outs),)),
        ],
        compiler_params=params(),
        cost_estimate=us(cost),
        name=name,
    )(*args)


def forecast_first(*args):
    n = ROWS_A[1]
    halo = jax.ShapeDtypeStruct((72, 512), F32)
    return forecast_call(
        first_rows_kernel, "forecast_first", SEG_A, n, n + 4, [piece(n)] * 4, [halo, halo], args, 5
    )


def forecast_inner(*args):
    n = ROWS_B[1]
    return forecast_call(
        inner_rows_kernel, "forecast_inner", SEG_B, n, n + 4, [piece(n)] * 4, [], args, 9
    )


def forecast_edge(*args):
    return forecast_call(
        edge_rows_kernel,
        "forecast_edge",
        SEG_C,
        NE,
        24,
        [piece(NE)] * 4,
        [],
        args,
        0.1,
    )


def dot_nt(a, b):
    return lax.dot_general(a, b, (((1,), (1,)), ((), ())), preferred_element_type=F32)


def weight_kernel(count, cell, value, var, land, out, sea_out):
    me = lax.axis_index("mem")
    odd = me & 1
    slots = cell.shape[2]
    rows64 = lax.broadcasted_iota(jnp.int32, (64, slots), 0)
    rows128 = lax.broadcasted_iota(jnp.int32, (128, slots), 0)
    slot = lax.broadcasted_iota(jnp.int32, (1, slots), 1)
    sea = land[:, pl.ds(pl.multiple_of(me * 128, 128), 128)].astype(F32)
    lane = lax.broadcasted_iota(jnp.int32, (64, 128), 1)
    turned = pltpu.roll(sea, 64, 1)
    seas = (jnp.where(lane < 64, sea, turned), jnp.where(lane < 64, turned, sea))
    for b in range(2):
        c = cell[0, b : b + 1, :]
        live = slot < count[0, b]
        w = jnp.where(live, 1.0 / var[0, b : b + 1, :], 0.0)
        u = w * value[0, b : b + 1, :]
        at_row = rows64 == ((c >> 6) & 63)
        at_lane = rows128 == (((c >> 12) << 6) | (c & 63))
        terms = []
        for v in (w, u):
            hi = v.astype(BF16).astype(F32)
            terms += [jnp.where(at_row, t, 0.0).astype(BF16) for t in (hi, v - hi)]
        lhs = jnp.concatenate(terms, axis=0)
        rhs = jnp.where(at_lane, 1.0, 0.0).astype(BF16)
        full = dot_nt(lhs, rhs)
        fs = b ^ odd
        for n in range(2):
            v = (full[128 * n : 128 * n + 64] + full[128 * n + 64 : 128 * n + 128]) * seas[b]
            out[fs, n, 0:48] = v[8:56]
            out[fs, n, 48:56] = v[0:8]
            out[fs, n, 56:64] = v[56:64]
        sea_out[b] = seas[b]


def cell_weights(count, cell, value, var, land):
    return pl.pallas_call(
        weight_kernel,
        out_shape=[
            jax.ShapeDtypeStruct((2, 2, 64, 128), F32),
            jax.ShapeDtypeStruct((2, 64, 128), F32),
        ],
        in_specs=[pl.BlockSpec(memory_space=pltpu.SMEM), VM, VM, VM, VM],
        out_specs=[VM, VM],
        compiler_params=params(),
        cost_estimate=us(0.1),
        name="cell_weights",
    )(count, cell, value, var, land)


def gauss(off):
    return jnp.exp(-(off * off) / (2.0 * LOC * LOC))


GR = 208


def gram_rows(pieces, s_out, mean_out, wu, rows, acc, fs, lh, rh, rl, xo, me):
    for k in range(4):
        at = pl.multiple_of((me ^ k) * ML, ML)
        xo[:, pl.ds(at, ML), :] = pieces[k][0]
    sub = lax.broadcasted_iota(jnp.int32, (8, 128), 0)
    c = (lax.broadcasted_iota(jnp.int32, (1, 128), 1) & 63).astype(F32)
    ec = [gauss(c - 31.5 - 64.0 * j) for j in (-1, 0, 1)]
    sub16 = lax.broadcasted_iota(jnp.int32, (16, 128), 0)
    for half in range(2):
        r = (sub + rows[half]).astype(F32)
        er = [gauss(r - 31.5 - 64.0 * i) for i in (-1, 0, 1)]
        w = wu[0, 0, 8 * half : 8 * half + 8, :]
        u = wu[0, 1, 8 * half : 8 * half + 8, :]
        wi = [w * e for e in er]
        ui = [u * e for e in er]
        for j8 in range(8):
            rr = 8 * half + j8
            x = xo[rr]
            mean = jnp.sum(x, axis=0, keepdims=True) * (1.0 / 64.0)
            mean_out[0, rr : rr + 1, :] = mean
            s = x - mean
            s_out[0, rr] = s
            cols = pl.ds(128 * rr, 128)
            drives = jnp.zeros((16, 128), F32)
            for i in range(3):
                wrow = wi[i][j8 : j8 + 1]
                hi, lo = two_terms(s * wrow)
                lh[pl.ds(64 * i, 64), cols] = hi
                lh[pl.ds(GR + 64 * i, 64), cols] = lo
                drives = jnp.where(sub16 == i, ui[i][j8 : j8 + 1] - wrow * mean, drives)
            hi, lo = two_terms(drives)
            lh[pl.ds(192, 16), cols] = hi
            lh[pl.ds(GR + 192, 16), cols] = lo
            for j in range(3):
                hi, lo = two_terms(s * ec[j])
                rh[pl.ds(64 * j, 64), cols] = hi
                rl[pl.ds(64 * j, 64), cols] = lo
    both = dot_nt(lh[...], rh[...])
    acc[fs] += both[0:GR] + both[GR : 2 * GR] + dot_nt(lh[0:GR, :], rl[...])


def gram_kernel(halves, groups, rows_of, stage, *refs):
    me = lax.axis_index("mem")
    odd = (me & 1) == 1
    g = pl.program_id(0)
    refs = list(refs)
    pieces = [refs.pop(0) for _ in range(4)]
    wu = refs.pop(0)
    acc_in = None
    if stage != "first":
        acc_in = refs.pop(0)
        del refs[0:2]
    acc, s_out, mean_out = (refs.pop(0) for _ in range(3))
    extra = [refs.pop(0) for _ in range({"border": 1, "last": 2}.get(stage, 0))]
    tmp = refs

    @pl.when(g == 0)
    def _():
        acc[...] = jnp.zeros_like(acc) if acc_in is None else acc_in[...]

    if len(halves) == 2:
        fs = g // groups
    else:
        fs = halves[0]
    gram_rows(pieces, s_out, mean_out, wu, rows_of(g % groups), acc, fs, *tmp, me)

    if stage == "border":

        @pl.when(g == groups - 1)
        def _():
            d = acc[0]
            extra[0][...] = jnp.where(odd, d[:, 128:192], d[:, 0:64])

    if stage == "last":

        @pl.when(g == groups - 1)
        def _():
            b0 = acc[me & 1]
            b1 = acc[1 - (me & 1)]
            extra[0][...] = jnp.concatenate(
                [b0[:, 64:128] + b1[:, 0:64], b0[:, 128:192] + b1[:, 64:128]], axis=1
            )
            extra[1][...] = jnp.where(odd, b0[:, 0:64], b1[:, 128:192])


def WHOLE(shape):
    return pl.BlockSpec(shape, lambda g: (0,) * len(shape))


def gram_call(stage, halves, groups, first, rows_of, pieces, wu, held, cost):
    fs_of = (lambda g: g // groups) if len(halves) == 2 else (lambda g: halves[0])
    grp = lambda g: g % groups
    ins = []
    at = lambda g: first + grp(g)
    ins += [pl.BlockSpec((1, 16, ML, 128), lambda g: (fs_of(g), grp(g), 0, 0))] * 4
    ins.append(pl.BlockSpec((1, 2, 16, 128), lambda g: (fs_of(g), 0, at(g), 0)))
    args = list(pieces) + [wu]
    acc_shape = (2, GR, 192)
    outs = [
        jax.ShapeDtypeStruct(acc_shape, F32),
        jax.ShapeDtypeStruct((2, BS, 64, 128), F32),
        jax.ShapeDtypeStruct((2, BS, 128), F32),
    ]
    out_specs = [
        WHOLE(acc_shape),
        pl.BlockSpec((1, 16, 64, 128), lambda g: (fs_of(g), at(g), 0, 0)),
        pl.BlockSpec((1, 16, 128), lambda g: (fs_of(g), at(g), 0)),
    ]
    aliases = {}
    if stage != "first":
        aliases = {len(args) + 1: 1, len(args) + 2: 2}
        ins += [WHOLE(acc_shape)] + [pl.BlockSpec(memory_space=pl.ANY)] * 2
        args += list(held)
    if stage == "border":
        outs += [jax.ShapeDtypeStruct((GR, 64), F32)]
        out_specs += [WHOLE((GR, 64))]
    if stage == "last":
        outs += [jax.ShapeDtypeStruct((GR, 128), F32), jax.ShapeDtypeStruct((GR, 64), F32)]
        out_specs += [WHOLE((GR, 128)), WHOLE((GR, 64))]
    return pl.pallas_call(
        functools.partial(gram_kernel, halves, groups, rows_of, stage),
        grid=(len(halves) * groups,),
        out_shape=outs,
        in_specs=ins,
        out_specs=out_specs,
        input_output_aliases=aliases,
        scratch_shapes=[
            pltpu.VMEM((2 * GR, 2048), BF16),
            pltpu.VMEM((192, 2048), BF16),
            pltpu.VMEM((192, 2048), BF16),
            pltpu.VMEM((16, 64, 128), F32),
        ],
        compiler_params=params(),
        cost_estimate=us(cost),
        name="gram_" + stage,
    )(*args)


def join_kernel(mid, core, border, down, own, up):
    odd = (lax.axis_index("mem") & 1) == 1
    c = core[...]
    b = border[...]
    q = mid[...] + jnp.concatenate([jnp.where(odd, c, b), jnp.where(odd, b, c)], axis=1)
    for i, ref in enumerate((down, own, up)):
        ref[0:64] = q[64 * i : 64 * i + 64]
        ref[64:72] = jnp.broadcast_to(q[192 + i : 193 + i], (8, 128))


def join(mid, core, border):
    one = jax.ShapeDtypeStruct((72, 128), F32)
    return pl.pallas_call(
        join_kernel,
        out_shape=[one, one, one],
        in_specs=[VM, VM, VM],
        out_specs=[VM, VM, VM],
        compiler_params=params(),
        cost_estimate=us(0.1),
        name="join_grams",
    )(mid, core, border)


def dot32(a, b):
    return lax.dot_general(
        a, b, (((1,), (0,)), ((), ())), precision=HIGHEST, preferred_element_type=F32
    )


def weights_of(gram, drive):
    n = gram.shape[0]
    eye = (
        lax.broadcasted_iota(jnp.int32, (n, n), 0) == lax.broadcasted_iota(jnp.int32, (n, n), 1)
    ).astype(F32)
    system = (n - 1.0) * eye + gram
    squares = jnp.sum(jnp.sum(system * system, axis=1, keepdims=True), axis=0, keepdims=True)
    frob = jnp.sqrt(squares)
    iterate = system / frob
    root = None
    for it in range(NSI):
        prod = iterate if root is None else dot32(root, iterate)
        corr = 1.5 * eye - 0.5 * prod
        if it < NSI - 1:
            iterate = dot32(iterate, corr)
        root = corr if root is None else dot32(corr, root)
    half = root / jnp.sqrt(frob)
    row = dot32(dot32(jnp.broadcast_to(drive, (8, n)), half), half)
    return jnp.sqrt(n - 1.0) * half + row[0:1]


YS = 68


def analysis_kernel(own, fromlow, fromhigh, s0, m0, s1, m1, sea, out, tt, rhs, ys):
    me = lax.axis_index("mem")
    odd = me & 1
    g = pl.program_id(0)

    @pl.when(g == 0)
    def _():
        tot = own[...] + fromlow[...] + fromhigh[...]
        for b in range(2):
            t = tot[:, 64 * b : 64 * b + 64]
            hi, lo = two_terms(weights_of(t[0:64], t[64:65]))
            tt[b] = jnp.concatenate([hi, hi, lo], axis=1)

    lane = lax.broadcasted_iota(jnp.int32, (64, 128), 1)
    for half, (s, mean) in enumerate(((s0, m0), (s1, m1))):
        upd = []
        for b in range(2):
            for rr in range(8):
                hi, lo = two_terms(s[b ^ odd, rr])
                cols = pl.ds(128 * rr, 128)
                rhs[half, b, 0:64, cols] = hi
                rhs[half, b, 64:128, cols] = lo
                rhs[half, b, 128:192, cols] = hi
            upd.append(
                lax.dot_general(
                    tt[b], rhs[half, b], (((1,), (0,)), ((), ())), preferred_element_type=F32
                )
            )
        for rr in range(8):
            res = []
            for b in range(2):
                x = s[b ^ odd, rr]
                up = upd[b][:, 128 * rr : 128 * rr + 128]
                m = mean[b ^ odd, rr : rr + 1, :]
                at = 8 * half + rr
                res.append((m + x) + sea[b, at : at + 1, :] * (up - x))
            at = pl.ds(YS * rr, 64)
            ys[half, 0, at, :] = jnp.where(lane < 64, res[0], pltpu.roll(res[1], 64, 1))
            ys[half, 1, at, :] = jnp.where(lane < 64, pltpu.roll(res[0], 64, 1), res[1])
        for m in range(64):
            for lev in range(2):
                out[m, lev, 8 * half : 8 * half + 8] = ys[half, lev, pl.ds(m, 8, stride=YS), :]


def kept_at(n):
    return jnp.where(n == 0, 6, jnp.where(n == 7, 7, n - 1))


def analysis(own, fromlow, fromhigh, s, mean, sea):
    ins = [WHOLE((72, 128))] * 3
    for half in range(2):
        at = lambda g, half=half: kept_at(2 * g + half)
        ins.append(pl.BlockSpec((2, 8, 64, 128), lambda g, at=at: (0, at(g), 0, 0)))
        ins.append(pl.BlockSpec((2, 8, 128), lambda g, at=at: (0, at(g), 0)))
    ins.append(pl.BlockSpec((2, 16, 128), lambda g: (0, g, 0)))
    return pl.pallas_call(
        analysis_kernel,
        grid=(4,),
        out_shape=jax.ShapeDtypeStruct((64, 2, 64, 128), F32),
        in_specs=ins,
        out_specs=pl.BlockSpec((64, 2, 16, 128), lambda g: (0, 0, g, 0)),
        scratch_shapes=[
            pltpu.VMEM((2, 64, 192), BF16),
            pltpu.VMEM((2, 2, 192, 1024), BF16),
            pltpu.VMEM((2, 2, 8 * YS, 128), F32),
        ],
        compiler_params=params(),
        cost_estimate=us(8),
        name="analysis",
    )(own, fromlow, fromhigh, s, mean, s, mean, sea)


def per_device(state, diffusivity, land_sea, obs_value, obs_var, obs_cell, obs_count):
    tiles = lax.axis_size("tile")
    up = [(i, i + 1) for i in range(tiles - 1)]
    down = [(i + 1, i) for i in range(tiles - 1)]
    swap = lambda k: [(i, i ^ k) for i in range(4)]

    mem = lambda v, k: lax.ppermute(v, "mem", swap(k))
    after = lax.optimization_barrier

    a = forecast_first(state, diffusivity, land_sea)
    a2, a3, a1 = mem(a[2], 2), mem(a[3], 3), mem(a[1], 1)
    land_b, hup, hdn = after((land_sea, a[4], a[5]))
    b = list(forecast_inner(state, diffusivity, land_b))
    hup, hdn, obs_cell, b[0] = after((hup, hdn, obs_cell, b[0]))
    b2, b3, b1 = mem(b[2], 2), mem(b[3], 3), mem(b[1], 1)
    above = lax.ppermute(hup, "tile", up)
    below = lax.ppermute(hdn, "tile", down)
    wu, sea = cell_weights(obs_count, obs_cell, obs_value, obs_var, land_sea)
    first = (a[0], a1, a2, a3)
    acc, s, mean = gram_call("first", (0, 1), 1, 0, lambda j: (8, 16), first, wu, None, 5)
    acc, land_e = after((acc, land_sea))
    e = list(forecast_edge(state, diffusivity, land_e, above, below))
    e2, e3, e1 = mem(e[2], 2), mem(e[3], 3), mem(e[1], 1)
    acc, e[0] = after((acc, e[0]))
    inner = (b[0], b1, b2, b3)
    edge = (e[0], e1, e2, e3)
    rows = lambda j: (16 * j + 24, 16 * j + 32)
    held = gram_call("inner", (0, 1), 2, 1, rows, inner, wu, (acc, s, mean), 9)
    *held, border = gram_call("border", (0,), 1, 3, lambda j: (0, 56), edge, wu, held, 3)
    border = lax.ppermute(border, "mem", [(1, 2), (2, 1)])
    _, s, mean, mid, core = gram_call(
        "last", (1,), 1, 3, lambda j: (0, 56), edge, wu, held, 0.1
    )
    core = mem(core, 1)
    to_low, own, to_high = join(mid, core, border)
    fromlow = lax.ppermute(to_high, "tile", up)
    fromhigh = lax.ppermute(to_low, "tile", down)
    return analysis(own, fromlow, fromhigh, s, mean, sea)


def solution(mesh):
    return jax.shard_map(
        per_device,
        mesh=mesh,
        in_specs=(
            P("mem", None, "tile", None),
            P("tile", None),
            P("tile", None),
            P("tile", "mem", None),
            P("tile", "mem", None),
            P("tile", "mem", None),
            P("tile", "mem"),
        ),
        out_specs=P(None, None, "tile", "mem"),
        check_vma=False,
    )
```

```python
import functools

import jax
import jax.numpy as jnp
from jax import lax
from jax.experimental import pallas as pl
from jax.experimental.pallas import tpu as pltpu
from jax.sharding import PartitionSpec as P

NSI = 4
LOC = 48.0
BS = 64
UNROLL = 4
UNROLL_B = 6
ML = 16
NE = 16
F32 = jnp.float32
BF16 = jnp.bfloat16
VMEM_LIMIT = 56 * 1024 * 1024
HIGHEST = lax.Precision.HIGHEST


def params(**kw):
    return pltpu.CompilerParams(vmem_limit_bytes=VMEM_LIMIT, **kw)


def two_terms(x):
    hi = x.astype(BF16)
    lo = (x - hi.astype(F32)).astype(BF16)
    return hi, lo


def pack_store(zs, z, row, lane):
    low = lane < 64
    for q in range(4):
        r0 = pltpu.roll(z[0][q], 64, 1)
        r1 = pltpu.roll(z[1][q], 64, 1)
        pair = (jnp.where(low, z[0][q], r1), jnp.where(low, r0, z[1][q]))
        for b in range(2):
            zs[q, b ^ (q & 1), row] = pair[b]


def fill_md(md, dif, land, rows):
    for r8 in sorted({r // 8 for r in rows}):
        m = land[8 * r8 : 8 * r8 + 8, :].astype(F32) * dif[8 * r8 : 8 * r8 + 8, :]
        for j in range(8):
            if 8 * r8 + j in rows:
                for q in range(4):
                    md[8 * r8 + j, q] = jnp.broadcast_to(
                        m[j : j + 1, 128 * q : 128 * q + 128], (8, 128)
                    )


def md_row(md, r):
    return [jnp.concatenate([md[r, q], md[r, q]], axis=0) for q in range(4)]


class Rows:
    def __init__(self, state, xs, sems, segments):
        self.n = sum(length for _, length in segments)
        self.stride = 2 * self.n + 8
        self.flat = xs.reshape(4 * ML * self.stride, 128)
        self.segments = segments
        self.copies = []
        for lev in range(2):
            todo = []
            at = 0
            for i, (start, length) in enumerate(segments):
                for q in range(4):
                    todo.append(
                        pltpu.make_async_copy(
                            state.at[:, lev, pl.ds(start, length), pl.ds(128 * q, 128)],
                            xs.at[q, :, pl.ds(lev * self.n + at, length)],
                            sems.at[lev, i * 4 + q],
                        )
                    )
                at += length
            self.copies.append(todo)

    def start(self):
        for todo in self.copies:
            for c in todo:
                c.start()

    def wait(self, lev):
        for c in self.copies[lev]:
            c.wait()

    def offset(self, r):
        at = 0
        for start, length in self.segments:
            if start <= r < start + length:
                return r - start + at
            at += length
        raise ValueError(r)

    def load(self, lev, off):
        return [
            self.flat[pl.ds(q * ML * self.stride + lev * self.n + off, ML, stride=self.stride), :]
            for q in range(4)
        ]


class Stencil:
    def __init__(self, x, y):
        self.x = x
        self.y = y
        self.lane = lax.broadcasted_iota(jnp.int32, (ML, 128), 1)

    def put(self, ref, p, lev, tiles):
        for q in range(4):
            ref[p, lev, :, pl.ds(128 * q, 128)] = tiles[q]

    def step(self, ref, p, lev, md):
        mid = [ref[p, lev, :, pl.ds(128 * q, 128)] for q in range(4)]
        fwd = [pltpu.roll(t, 1, 1) for t in mid]
        bwd = [pltpu.roll(t, 127, 1) for t in mid]
        zero = jnp.zeros_like(mid[0])
        out = []
        for q in range(4):
            cols = pl.ds(128 * q, 128)
            left = jnp.where(self.lane == 0, fwd[q - 1] if q > 0 else zero, fwd[q])
            right = jnp.where(self.lane == 127, bwd[q + 1] if q < 3 else zero, bwd[q])
            near = (ref[p - 1, lev, :, cols] + ref[p + 1, lev, :, cols]) + (left + right)
            out.append(mid[q] + md[q] * (near - 4.0 * mid[q]))
        return out


class Sender:
    def __init__(self, zs, outs, me, sems):
        self.zs = zs
        self.outs = outs
        self.me = me
        self.sems = sems
        self.copies = []

    def send(self, at, length):
        for k in range(4):
            c = pltpu.make_async_copy(
                self.zs.at[self.me ^ k, :, pl.ds(at, length)],
                self.outs[k].at[:, pl.ds(at, length)],
                self.sems.at[len(self.copies)],
            )
            c.start()
            self.copies.append(c)

    def wait(self):
        for c in self.copies:
            c.wait()


SEG_A = ((0, 8), (16, 48))
SEG_B = ((0, 32),)
SEG_C = ((0, 16), (48, 16))
ROWS_A = (24, 32)
ROWS_B = (8, 16)


def plain_rows(rows, st, md, zs, sender, r0, n):
    off = rows.offset(r0 - 2)
    lane = lax.broadcasted_iota(jnp.int32, (ML, 128), 1)
    for lev in range(2):
        rows.wait(lev)

        @pl.loop(0, n + 4, unroll=2)
        def _(p, lev=lev):
            st.put(st.x, p, lev, rows.load(lev, off + p))

    @pl.loop(1, n + 3, unroll=UNROLL_B)
    def _(p):
        m = md_row(md, p + (r0 - 2))
        for lev in range(2):
            st.put(st.y, p, lev, st.step(st.x, p, lev, m))

    for blk in range(n // 8):

        @pl.loop(8 * blk, 8 * blk + 8, unroll=UNROLL)
        def _(i):
            m = md_row(md, i + r0)
            pack_store(zs, [st.step(st.y, i + 2, lev, m) for lev in range(2)], i, lane)

        sender.send(8 * blk, 8)
    sender.wait()


def first_rows_kernel(
    state, dif, land, o0, o1, o2, o3, hup, hdn, xs, zs, md, x, y, isem, osem
):
    rows = Rows(state, xs, isem, SEG_A)
    rows.start()
    r0, n = ROWS_A
    fill_md(md, dif, land, [0, 63, *range(r0 - 1, r0 + n + 1)])
    st = Stencil(x, y)
    sender = Sender(zs, (o0, o1, o2, o3), lax.axis_index("mem"), osem)
    plain_rows(rows, st, md, zs, sender, r0, n)
    for j in range(2):
        for lev in range(2):
            for ref, r in ((hdn, j), (hup, 62 + j)):
                v = rows.load(lev, rows.offset(r))
                for q in range(4):
                    ref[pl.ds(j * 32 + lev * 16, 16), pl.ds(128 * q, 128)] = v[q]
    for ref, r in ((hup, 63), (hdn, 0)):
        for q in range(4):
            ref[64:72, 128 * q : 128 * q + 128] = md[r, q]


def inner_rows_kernel(
    state, dif, land, o0, o1, o2, o3, xs, zs, md, x, y, isem, osem
):
    rows = Rows(state, xs, isem, SEG_B)
    rows.start()
    r0, n = ROWS_B
    fill_md(md, dif, land, range(r0 - 1, r0 + n + 1))
    st = Stencil(x, y)
    sender = Sender(zs, (o0, o1, o2, o3), lax.axis_index("mem"), osem)
    plain_rows(rows, st, md, zs, sender, r0, n)


def edge_rows_kernel(
    state, dif, land, above, below, o0, o1, o2, o3, xs, zs, md, x, y, isem, osem
):
    rows = Rows(state, xs, isem, SEG_C)
    rows.start()
    fill_md(md, dif, land, [*range(9), *range(55, 64)])
    st = Stencil(x, y)
    sender = Sender(zs, (o0, o1, o2, o3), lax.axis_index("mem"), osem)
    lane = lax.broadcasted_iota(jnp.int32, (ML, 128), 1)
    for ref, p0 in ((above, 0), (below, 22)):
        for j in range(2):
            for lev in range(2):
                at = pl.ds(j * 32 + lev * 16, 16)
                st.put(x, p0 + j, lev, [ref[at, 128 * q : 128 * q + 128] for q in range(4)])
    for lev in range(2):
        rows.wait(lev)

        @pl.loop(0, 10, unroll=2)
        def _(i, lev=lev):
            st.put(x, i + 2, lev, rows.load(lev, i))
            st.put(x, i + 12, lev, rows.load(lev, i + 22))

    def outside(ref):
        tiles = [ref[64:72, 128 * q : 128 * q + 128] for q in range(4)]
        return [jnp.concatenate([t, t], axis=0) for t in tiles]

    for p, ref in ((1, above), (22, below)):
        for lev in range(2):
            st.put(y, p, lev, st.step(x, p, lev, outside(ref)))

    @pl.loop(0, 9, unroll=3)
    def _(i):
        m = md_row(md, i)
        w = md_row(md, i + 55)
        for lev in range(2):
            st.put(y, i + 2, lev, st.step(x, i + 2, lev, m))
            st.put(y, i + 13, lev, st.step(x, i + 13, lev, w))

    for blk in range(2):

        @pl.loop(0, 8, unroll=UNROLL)
        def _(i, blk=blk):
            m = md_row(md, i + 56 * blk)
            z = [st.step(y, i + 2 + 12 * blk, lev, m) for lev in range(2)]
            pack_store(zs, z, i + 8 * blk, lane)

        sender.send(8 * blk, 8)
    sender.wait()


ANY = pl.BlockSpec(memory_space=pl.ANY)
VM = pl.BlockSpec(memory_space=pltpu.VMEM)


def us(t):
    return pl.CostEstimate(
        flops=int(t * 1.1e9), bytes_accessed=int(t * 3.4e6), transcendentals=0
    )


def piece(n):
    return jax.ShapeDtypeStruct((2, n, ML, 128), F32)


def forecast_call(kernel, name, segments, n, count, outs, extra_out, args, cost):
    loaded = sum(length for _, length in segments)
    kept = (count, 2, ML, 512)
    return pl.pallas_call(
        kernel,
        out_shape=outs + extra_out,
        in_specs=[ANY] + [VM] * (len(args) - 1),
        out_specs=[ANY] * len(outs) + [VM] * len(extra_out),
        scratch_shapes=[
            pltpu.VMEM((4, ML, 2 * loaded + 8, 128), F32),
            pltpu.VMEM((4, 2, n, ML, 128), F32),
            pltpu.VMEM((64, 4, 8, 128), F32),
            pltpu.VMEM(kept, F32),
            pltpu.VMEM(kept, F32),
            pltpu.SemaphoreType.DMA((2, 4 * len(segments))),
            pltpu.SemaphoreType.DMA((n // 8 * len(outs),)),
        ],
        compiler_params=params(),
        cost_estimate=us(cost),
        name=name,
    )(*args)


def forecast_first(*args):
    n = ROWS_A[1]
    halo = jax.ShapeDtypeStruct((72, 512), F32)
    return forecast_call(
        first_rows_kernel, "forecast_first", SEG_A, n, n + 4, [piece(n)] * 4, [halo, halo], args, 5
    )


def forecast_inner(*args):
    n = ROWS_B[1]
    return forecast_call(
        inner_rows_kernel, "forecast_inner", SEG_B, n, n + 4, [piece(n)] * 4, [], args, 9
    )


def forecast_edge(*args):
    return forecast_call(
        edge_rows_kernel,
        "forecast_edge",
        SEG_C,
        NE,
        24,
        [piece(NE)] * 4,
        [],
        args,
        0.1,
    )


def dot_nt(a, b):
    return lax.dot_general(a, b, (((1,), (1,)), ((), ())), preferred_element_type=F32)


def weight_kernel(count, cell, value, var, land, out, sea_out):
    me = lax.axis_index("mem")
    odd = me & 1
    slots = cell.shape[2]
    rows64 = lax.broadcasted_iota(jnp.int32, (64, slots), 0)
    rows128 = lax.broadcasted_iota(jnp.int32, (128, slots), 0)
    slot = lax.broadcasted_iota(jnp.int32, (1, slots), 1)
    sea = land[:, pl.ds(pl.multiple_of(me * 128, 128), 128)].astype(F32)
    lane = lax.broadcasted_iota(jnp.int32, (64, 128), 1)
    turned = pltpu.roll(sea, 64, 1)
    seas = (jnp.where(lane < 64, sea, turned), jnp.where(lane < 64, turned, sea))
    for b in range(2):
        c = cell[0, b : b + 1, :]
        live = slot < count[0, b]
        w = jnp.where(live, 1.0 / var[0, b : b + 1, :], 0.0)
        u = w * value[0, b : b + 1, :]
        at_row = rows64 == ((c >> 6) & 63)
        at_lane = rows128 == (((c >> 12) << 6) | (c & 63))
        terms = []
        for v in (w, u):
            hi = v.astype(BF16).astype(F32)
            terms += [jnp.where(at_row, t, 0.0).astype(BF16) for t in (hi, v - hi)]
        lhs = jnp.concatenate(terms, axis=0)
        rhs = jnp.where(at_lane, 1.0, 0.0).astype(BF16)
        full = dot_nt(lhs, rhs)
        fs = b ^ odd
        for n in range(2):
            v = (full[128 * n : 128 * n + 64] + full[128 * n + 64 : 128 * n + 128]) * seas[b]
            out[fs, n, 0:48] = v[8:56]
            out[fs, n, 48:56] = v[0:8]
            out[fs, n, 56:64] = v[56:64]
        sea_out[b] = seas[b]


def cell_weights(count, cell, value, var, land):
    return pl.pallas_call(
        weight_kernel,
        out_shape=[
            jax.ShapeDtypeStruct((2, 2, 64, 128), F32),
            jax.ShapeDtypeStruct((2, 64, 128), F32),
        ],
        in_specs=[pl.BlockSpec(memory_space=pltpu.SMEM), VM, VM, VM, VM],
        out_specs=[VM, VM],
        compiler_params=params(),
        cost_estimate=us(0.1),
        name="cell_weights",
    )(count, cell, value, var, land)


def gauss(off):
    return jnp.exp(-(off * off) / (2.0 * LOC * LOC))


GR = 208


def gram_rows(pieces, s_out, mean_out, wu, rows, acc, fs, lh, rh, rl, xo, me):
    for k in range(4):
        at = pl.multiple_of((me ^ k) * ML, ML)
        xo[:, pl.ds(at, ML), :] = pieces[k][0]
    sub = lax.broadcasted_iota(jnp.int32, (8, 128), 0)
    c = (lax.broadcasted_iota(jnp.int32, (1, 128), 1) & 63).astype(F32)
    ec = [gauss(c - 31.5 - 64.0 * j) for j in (-1, 0, 1)]
    sub16 = lax.broadcasted_iota(jnp.int32, (16, 128), 0)
    for half in range(len(rows)):
        r = (sub + rows[half]).astype(F32)
        er = [gauss(r - 31.5 - 64.0 * i) for i in (-1, 0, 1)]
        w = wu[0, 0, 8 * half : 8 * half + 8, :]
        u = wu[0, 1, 8 * half : 8 * half + 8, :]
        wi = [w * e for e in er]
        ui = [u * e for e in er]
        for j8 in range(8):
            rr = 8 * half + j8
            x = xo[rr]
            mean = jnp.sum(x, axis=0, keepdims=True) * (1.0 / 64.0)
            mean_out[0, rr : rr + 1, :] = mean
            s = x - mean
            s_out[0, rr] = s
            cols = pl.ds(128 * rr, 128)
            drives = jnp.zeros((16, 128), F32)
            for i in range(3):
                wrow = wi[i][j8 : j8 + 1]
                hi, lo = two_terms(s * wrow)
                lh[pl.ds(64 * i, 64), cols] = hi
                lh[pl.ds(GR + 64 * i, 64), cols] = lo
                drives = jnp.where(sub16 == i, ui[i][j8 : j8 + 1] - wrow * mean, drives)
            hi, lo = two_terms(drives)
            lh[pl.ds(192, 16), cols] = hi
            lh[pl.ds(GR + 192, 16), cols] = lo
            for j in range(3):
                hi, lo = two_terms(s * ec[j])
                rh[pl.ds(64 * j, 64), cols] = hi
                rl[pl.ds(64 * j, 64), cols] = lo
    both = dot_nt(lh[...], rh[...])
    acc[fs] += both[0:GR] + both[GR : 2 * GR] + dot_nt(lh[0:GR, :], rl[...])


def gram_kernel(halves, groups, rows, stage, *refs):
    me = lax.axis_index("mem")
    odd = (me & 1) == 1
    g = pl.program_id(0)
    refs = list(refs)
    pieces = [refs.pop(0) for _ in range(4)]
    wu = refs.pop(0)
    acc_in = None
    if stage != "first":
        acc_in = refs.pop(0)
        del refs[0:2]
    acc, s_out, mean_out = (refs.pop(0) for _ in range(3))
    extra = [refs.pop(0) for _ in range({"border": 1, "last": 2}.get(stage, 0))]
    tmp = refs

    @pl.when(g == 0)
    def _():
        acc[...] = jnp.zeros_like(acc) if acc_in is None else acc_in[...]

    if len(halves) == 2:
        fs = g // groups
    else:
        fs = halves[0]
    first = [r + 16 * (g % groups) for r in rows]
    gram_rows(pieces, s_out, mean_out, wu, first, acc, fs, *tmp, me)

    if stage == "border":

        @pl.when(g == len(halves) * groups - 1)
        def _():
            d = acc[0]
            extra[0][...] = jnp.where(odd, d[:, 128:192], d[:, 0:64])

    if stage == "last":

        @pl.when(g == len(halves) * groups - 1)
        def _():
            b0 = acc[me & 1]
            b1 = acc[1 - (me & 1)]
            extra[0][...] = jnp.concatenate(
                [b0[:, 64:128] + b1[:, 0:64], b0[:, 128:192] + b1[:, 64:128]], axis=1
            )
            extra[1][...] = jnp.where(odd, b0[:, 0:64], b1[:, 128:192])


def WHOLE(shape):
    return pl.BlockSpec(shape, lambda g: (0,) * len(shape))


def gram_call(stage, halves, groups, kept, rows, pieces, wu, held, cost):
    n = 16
    fs_of = (lambda g: g // groups) if len(halves) == 2 else (lambda g: halves[0])
    sub = lambda g: g % groups
    ins = [pl.BlockSpec((1, n, ML, 128), lambda g: (fs_of(g), sub(g), 0, 0))] * 4
    ins.append(pl.BlockSpec((1, 2, n, 128), lambda g: (fs_of(g), 0, kept + sub(g), 0)))
    args = list(pieces) + [wu]
    acc_shape = (2, GR, 192)
    outs = [
        jax.ShapeDtypeStruct(acc_shape, F32),
        jax.ShapeDtypeStruct((2, BS, 64, 128), F32),
        jax.ShapeDtypeStruct((2, BS, 128), F32),
    ]
    out_specs = [
        WHOLE(acc_shape),
        pl.BlockSpec((1, n, 64, 128), lambda g: (fs_of(g), kept + sub(g), 0, 0)),
        pl.BlockSpec((1, n, 128), lambda g: (fs_of(g), kept + sub(g), 0)),
    ]
    aliases = {}
    if stage != "first":
        aliases = {len(args) + 1: 1, len(args) + 2: 2}
        ins += [WHOLE(acc_shape)] + [pl.BlockSpec(memory_space=pl.ANY)] * 2
        args += list(held)
    if stage == "border":
        outs += [jax.ShapeDtypeStruct((GR, 64), F32)]
        out_specs += [WHOLE((GR, 64))]
    if stage == "last":
        outs += [jax.ShapeDtypeStruct((GR, 128), F32), jax.ShapeDtypeStruct((GR, 64), F32)]
        out_specs += [WHOLE((GR, 128)), WHOLE((GR, 64))]
    return pl.pallas_call(
        functools.partial(gram_kernel, halves, groups, rows, stage),
        grid=(len(halves) * groups,),
        out_shape=outs,
        in_specs=ins,
        out_specs=out_specs,
        input_output_aliases=aliases,
        scratch_shapes=[
            pltpu.VMEM((2 * GR, 128 * n), BF16),
            pltpu.VMEM((192, 128 * n), BF16),
            pltpu.VMEM((192, 128 * n), BF16),
            pltpu.VMEM((n, 64, 128), F32),
        ],
        compiler_params=params(),
        cost_estimate=us(cost),
        name="gram_" + stage,
    )(*args)


def join_kernel(mid, core, border, down, own, up):
    odd = (lax.axis_index("mem") & 1) == 1
    c = core[...]
    b = border[...]
    q = mid[...] + jnp.concatenate([jnp.where(odd, c, b), jnp.where(odd, b, c)], axis=1)
    for i, ref in enumerate((down, own, up)):
        ref[0:64] = q[64 * i : 64 * i + 64]
        ref[64:72] = jnp.broadcast_to(q[192 + i : 193 + i], (8, 128))


def join(mid, core, border):
    one = jax.ShapeDtypeStruct((72, 128), F32)
    return pl.pallas_call(
        join_kernel,
        out_shape=[one, one, one],
        in_specs=[VM, VM, VM],
        out_specs=[VM, VM, VM],
        compiler_params=params(),
        cost_estimate=us(0.1),
        name="join_grams",
    )(mid, core, border)


def dot32(a, b):
    return lax.dot_general(
        a, b, (((1,), (0,)), ((), ())), precision=HIGHEST, preferred_element_type=F32
    )


def weights_of(gram, drive):
    n = gram.shape[0]
    eye = (
        lax.broadcasted_iota(jnp.int32, (n, n), 0) == lax.broadcasted_iota(jnp.int32, (n, n), 1)
    ).astype(F32)
    system = (n - 1.0) * eye + gram
    squares = jnp.sum(jnp.sum(system * system, axis=1, keepdims=True), axis=0, keepdims=True)
    frob = jnp.sqrt(squares)
    iterate = system / frob
    root = None
    for it in range(NSI):
        prod = iterate if root is None else dot32(root, iterate)
        corr = 1.5 * eye - 0.5 * prod
        if it < NSI - 1:
            iterate = dot32(iterate, corr)
        root = corr if root is None else dot32(corr, root)
    half = root / jnp.sqrt(frob)
    row = dot32(dot32(jnp.broadcast_to(drive, (8, n)), half), half)
    return jnp.sqrt(n - 1.0) * half + row[0:1]


YS = 68


def kept_at(n):
    return jnp.where(n == 0, 6, jnp.where(n == 7, 7, n - 1)) * 8


def analysis_kernel(
    own, fromlow, fromhigh, mean, sea, spread, out, sv, tt, rhs, ys, ov, isem, osem
):
    me = lax.axis_index("mem")
    odd = me & 1

    def fetch(n):
        rows = pl.ds(pl.multiple_of(kept_at(n), 8), 8)
        return pltpu.make_async_copy(spread.at[:, rows], sv.at[n], isem.at[n])

    def store(half, n):
        rows = pl.ds(pl.multiple_of(8 * n, 8), 8)
        return pltpu.make_async_copy(ov.at[half], out.at[:, :, rows], osem.at[half])

    for n in range(8):
        fetch(jnp.int32(n)).start()
    tot = own[...] + fromlow[...] + fromhigh[...]
    for b in range(2):
        t = tot[:, 64 * b : 64 * b + 64]
        hi, lo = two_terms(weights_of(t[0:64], t[64:65]))
        tt[b] = jnp.concatenate([hi, hi, lo], axis=1)
    lane = lax.broadcasted_iota(jnp.int32, (64, 128), 1)

    @pl.loop(0, 4)
    def _(i):
        for half in range(2):
            n = 2 * i + half
            fetch(n).wait()
            upd = []
            for b in range(2):
                for rr in range(8):
                    hi, lo = two_terms(sv[n, b ^ odd, rr])
                    cols = pl.ds(128 * rr, 128)
                    rhs[half, b, 0:64, cols] = hi
                    rhs[half, b, 64:128, cols] = lo
                    rhs[half, b, 128:192, cols] = hi
                upd.append(
                    lax.dot_general(
                        tt[b], rhs[half, b], (((1,), (0,)), ((), ())), preferred_element_type=F32
                    )
                )
            m8 = [
                mean[b ^ odd, pl.ds(pl.multiple_of(kept_at(n), 8), 8), :] for b in range(2)
            ]
            sea8 = [sea[b, pl.ds(pl.multiple_of(8 * n, 8), 8), :] for b in range(2)]
            for rr in range(8):
                res = []
                for b in range(2):
                    x = sv[n, b ^ odd, rr]
                    up = upd[b][:, 128 * rr : 128 * rr + 128]
                    res.append((m8[b][rr : rr + 1] + x) + sea8[b][rr : rr + 1] * (up - x))
                at = pl.ds(YS * rr, 64)
                ys[half, 0, at, :] = jnp.where(lane < 64, res[0], pltpu.roll(res[1], 64, 1))
                ys[half, 1, at, :] = jnp.where(lane < 64, pltpu.roll(res[0], 64, 1), res[1])

            @pl.when(i > 0)
            def _(half=half, n=n):
                store(half, n).wait()

            for m in range(64):
                for lev in range(2):
                    ov[half, m, lev] = ys[half, lev, pl.ds(m, 8, stride=YS), :]
            store(half, n).start()

    for half in range(2):
        store(half, jnp.int32(6 + half)).wait()


def analysis(own, fromlow, fromhigh, s, mean, sea):
    return pl.pallas_call(
        analysis_kernel,
        out_shape=jax.ShapeDtypeStruct((64, 2, 64, 128), F32),
        in_specs=[VM] * 5 + [ANY],
        out_specs=ANY,
        scratch_shapes=[
            pltpu.VMEM((8, 2, 8, 64, 128), F32),
            pltpu.VMEM((2, 64, 192), BF16),
            pltpu.VMEM((2, 2, 192, 1024), BF16),
            pltpu.VMEM((2, 2, 8 * YS, 128), F32),
            pltpu.VMEM((2, 64, 2, 8, 128), F32),
            pltpu.SemaphoreType.DMA((8,)),
            pltpu.SemaphoreType.DMA((2,)),
        ],
        compiler_params=params(),
        cost_estimate=us(8),
        name="analysis",
    )(own, fromlow, fromhigh, mean, sea, s)


def per_device(state, diffusivity, land_sea, obs_value, obs_var, obs_cell, obs_count):
    tiles = lax.axis_size("tile")
    up = [(i, i + 1) for i in range(tiles - 1)]
    down = [(i + 1, i) for i in range(tiles - 1)]
    swap = lambda k: [(i, i ^ k) for i in range(4)]

    mem = lambda v, k: lax.ppermute(v, "mem", swap(k))
    after = lax.optimization_barrier

    a = list(forecast_first(state, diffusivity, land_sea))
    a2, a3, a1 = mem(a[2], 2), mem(a[3], 3), mem(a[1], 1)
    hup, hdn, a1 = after((a[4], a[5], a1))
    above = lax.ppermute(hup, "tile", up)
    below = lax.ppermute(hdn, "tile", down)
    a[0], land_b = after((a[0], land_sea))
    b = list(forecast_inner(state, diffusivity, land_b))
    b2, b3, b1 = mem(b[2], 2), mem(b[3], 3), mem(b[1], 1)
    land_e, b[0] = after((land_sea, b[0]))
    e = list(forecast_edge(state, diffusivity, land_e, above, below))
    e2, e3, e1 = mem(e[2], 2), mem(e[3], 3), mem(e[1], 1)
    obs_cell, e1 = after((obs_cell, e1))
    wu, sea = cell_weights(obs_count, obs_cell, obs_value, obs_var, land_sea)
    held = gram_call("first", (0, 1), 2, 1, (24, 32), (a[0], a1, a2, a3), wu, None, 0.1)
    held = gram_call("inner", (0, 1), 1, 0, (8, 16), (b[0], b1, b2, b3), wu, held, 0.1)
    edge = (e[0], e1, e2, e3)
    *held, border = gram_call("border", (0,), 1, 3, (0, 56), edge, wu, held, 3)
    border = lax.ppermute(border, "mem", [(1, 2), (2, 1)])
    _, s, mean, mid, core = gram_call("last", (1,), 1, 3, (0, 56), edge, wu, held, 4)
    core, border = after((core, border))
    core = mem(core, 1)
    to_low, own, to_high = join(mid, core, border)
    fromlow = lax.ppermute(to_high, "tile", up)
    fromhigh = lax.ppermute(to_low, "tile", down)
    return analysis(own, fromlow, fromhigh, s, mean, sea)


def solution(mesh):
    return jax.shard_map(
        per_device,
        mesh=mesh,
        in_specs=(
            P("mem", None, "tile", None),
            P("tile", None),
            P("tile", None),
            P("tile", "mem", None),
            P("tile", "mem", None),
            P("tile", "mem", None),
            P("tile", "mem"),
        ),
        out_specs=P(None, None, "tile", "mem"),
        check_vma=False,
    )
```

```python
import functools

import jax
import jax.numpy as jnp
from jax import lax
from jax.experimental import pallas as pl
from jax.experimental.pallas import tpu as pltpu
from jax.sharding import PartitionSpec as P

NSI = 4
LOC = 48.0
BS = 64
UNROLL = 4
UNROLL_B = 6
ML = 16
NE = 16
F32 = jnp.float32
BF16 = jnp.bfloat16
VMEM_LIMIT = 56 * 1024 * 1024
HIGHEST = lax.Precision.HIGHEST


def params(**kw):
    return pltpu.CompilerParams(vmem_limit_bytes=VMEM_LIMIT, **kw)


def two_terms(x):
    hi = x.astype(BF16)
    lo = (x - hi.astype(F32)).astype(BF16)
    return hi, lo


def pack_store(zs, z, row, lane):
    low = lane < 64
    for q in range(4):
        r0 = pltpu.roll(z[0][q], 64, 1)
        r1 = pltpu.roll(z[1][q], 64, 1)
        pair = (jnp.where(low, z[0][q], r1), jnp.where(low, r0, z[1][q]))
        for b in range(2):
            zs[q, b ^ (q & 1), row] = pair[b]


def fill_md(md, dif, land, rows):
    for r8 in sorted({r // 8 for r in rows}):
        m = land[8 * r8 : 8 * r8 + 8, :].astype(F32) * dif[8 * r8 : 8 * r8 + 8, :]
        for j in range(8):
            if 8 * r8 + j in rows:
                for q in range(4):
                    md[8 * r8 + j, q] = jnp.broadcast_to(
                        m[j : j + 1, 128 * q : 128 * q + 128], (8, 128)
                    )


def md_row(md, r):
    return [jnp.concatenate([md[r, q], md[r, q]], axis=0) for q in range(4)]


class Rows:
    def __init__(self, state, xs, sems, segments):
        self.n = sum(length for _, length in segments)
        self.stride = 2 * self.n + 8
        self.flat = xs.reshape(4 * ML * self.stride, 128)
        self.segments = segments
        self.copies = []
        for lev in range(2):
            todo = []
            at = 0
            for i, (start, length) in enumerate(segments):
                for q in range(4):
                    todo.append(
                        pltpu.make_async_copy(
                            state.at[:, lev, pl.ds(start, length), pl.ds(128 * q, 128)],
                            xs.at[q, :, pl.ds(lev * self.n + at, length)],
                            sems.at[lev, i * 4 + q],
                        )
                    )
                at += length
            self.copies.append(todo)

    def start(self):
        for todo in self.copies:
            for c in todo:
                c.start()

    def wait(self, lev):
        for c in self.copies[lev]:
            c.wait()

    def offset(self, r):
        at = 0
        for start, length in self.segments:
            if start <= r < start + length:
                return r - start + at
            at += length
        raise ValueError(r)

    def load(self, lev, off):
        return [
            self.flat[pl.ds(q * ML * self.stride + lev * self.n + off, ML, stride=self.stride), :]
            for q in range(4)
        ]


class Stencil:
    def __init__(self, x, y):
        self.x = x
        self.y = y
        self.lane = lax.broadcasted_iota(jnp.int32, (ML, 128), 1)

    def put(self, ref, p, lev, tiles):
        for q in range(4):
            ref[p, lev, :, pl.ds(128 * q, 128)] = tiles[q]

    def step(self, ref, p, lev, md):
        mid = [ref[p, lev, :, pl.ds(128 * q, 128)] for q in range(4)]
        fwd = [pltpu.roll(t, 1, 1) for t in mid]
        bwd = [pltpu.roll(t, 127, 1) for t in mid]
        zero = jnp.zeros_like(mid[0])
        out = []
        for q in range(4):
            cols = pl.ds(128 * q, 128)
            left = jnp.where(self.lane == 0, fwd[q - 1] if q > 0 else zero, fwd[q])
            right = jnp.where(self.lane == 127, bwd[q + 1] if q < 3 else zero, bwd[q])
            near = (ref[p - 1, lev, :, cols] + ref[p + 1, lev, :, cols]) + (left + right)
            out.append(mid[q] + md[q] * (near - 4.0 * mid[q]))
        return out


class Sender:
    def __init__(self, zs, outs, me, sems):
        self.zs = zs
        self.outs = outs
        self.me = me
        self.sems = sems
        self.copies = []

    def send(self, at, length):
        for k in range(4):
            c = pltpu.make_async_copy(
                self.zs.at[self.me ^ k, :, pl.ds(at, length)],
                self.outs[k].at[:, pl.ds(at, length)],
                self.sems.at[len(self.copies)],
            )
            c.start()
            self.copies.append(c)

    def wait(self):
        for c in self.copies:
            c.wait()


SEG_A = ((0, 8), (16, 48))
SEG_B = ((0, 32),)
SEG_C = ((0, 16), (48, 16))
ROWS_A = (24, 32)
ROWS_B = (8, 16)


def plain_rows(rows, st, md, zs, sender, r0, n):
    off = rows.offset(r0 - 2)
    lane = lax.broadcasted_iota(jnp.int32, (ML, 128), 1)
    for lev in range(2):
        rows.wait(lev)

        @pl.loop(0, n + 4, unroll=2)
        def _(p, lev=lev):
            st.put(st.x, p, lev, rows.load(lev, off + p))

    @pl.loop(1, n + 3, unroll=UNROLL_B)
    def _(p):
        m = md_row(md, p + (r0 - 2))
        for lev in range(2):
            st.put(st.y, p, lev, st.step(st.x, p, lev, m))

    for blk in range(n // 8):

        @pl.loop(8 * blk, 8 * blk + 8, unroll=UNROLL)
        def _(i):
            m = md_row(md, i + r0)
            pack_store(zs, [st.step(st.y, i + 2, lev, m) for lev in range(2)], i, lane)

        sender.send(8 * blk, 8)
    sender.wait()


def first_rows_kernel(
    state, dif, land, o0, o1, o2, o3, hup, hdn, xs, zs, md, x, y, isem, osem
):
    rows = Rows(state, xs, isem, SEG_A)
    rows.start()
    r0, n = ROWS_A
    fill_md(md, dif, land, [0, 63, *range(r0 - 1, r0 + n + 1)])
    st = Stencil(x, y)
    sender = Sender(zs, (o0, o1, o2, o3), lax.axis_index("mem"), osem)
    plain_rows(rows, st, md, zs, sender, r0, n)
    for j in range(2):
        for lev in range(2):
            for ref, r in ((hdn, j), (hup, 62 + j)):
                v = rows.load(lev, rows.offset(r))
                for q in range(4):
                    ref[pl.ds(j * 32 + lev * 16, 16), pl.ds(128 * q, 128)] = v[q]
    for ref, r in ((hup, 63), (hdn, 0)):
        for q in range(4):
            ref[64:72, 128 * q : 128 * q + 128] = md[r, q]


def inner_rows_kernel(
    state, dif, land, o0, o1, o2, o3, xs, zs, md, x, y, isem, osem
):
    rows = Rows(state, xs, isem, SEG_B)
    rows.start()
    r0, n = ROWS_B
    fill_md(md, dif, land, range(r0 - 1, r0 + n + 1))
    st = Stencil(x, y)
    sender = Sender(zs, (o0, o1, o2, o3), lax.axis_index("mem"), osem)
    plain_rows(rows, st, md, zs, sender, r0, n)


def edge_rows_kernel(
    state, dif, land, above, below, o0, o1, o2, o3, xs, zs, md, x, y, isem, osem
):
    rows = Rows(state, xs, isem, SEG_C)
    rows.start()
    fill_md(md, dif, land, [*range(9), *range(55, 64)])
    st = Stencil(x, y)
    sender = Sender(zs, (o0, o1, o2, o3), lax.axis_index("mem"), osem)
    lane = lax.broadcasted_iota(jnp.int32, (ML, 128), 1)
    for ref, p0 in ((above, 0), (below, 22)):
        for j in range(2):
            for lev in range(2):
                at = pl.ds(j * 32 + lev * 16, 16)
                st.put(x, p0 + j, lev, [ref[at, 128 * q : 128 * q + 128] for q in range(4)])
    for lev in range(2):
        rows.wait(lev)

        @pl.loop(0, 10, unroll=2)
        def _(i, lev=lev):
            st.put(x, i + 2, lev, rows.load(lev, i))
            st.put(x, i + 12, lev, rows.load(lev, i + 22))

    def outside(ref):
        tiles = [ref[64:72, 128 * q : 128 * q + 128] for q in range(4)]
        return [jnp.concatenate([t, t], axis=0) for t in tiles]

    for p, ref in ((1, above), (22, below)):
        for lev in range(2):
            st.put(y, p, lev, st.step(x, p, lev, outside(ref)))

    @pl.loop(0, 9, unroll=3)
    def _(i):
        m = md_row(md, i)
        w = md_row(md, i + 55)
        for lev in range(2):
            st.put(y, i + 2, lev, st.step(x, i + 2, lev, m))
            st.put(y, i + 13, lev, st.step(x, i + 13, lev, w))

    for blk in range(2):

        @pl.loop(0, 8, unroll=UNROLL)
        def _(i, blk=blk):
            m = md_row(md, i + 56 * blk)
            z = [st.step(y, i + 2 + 12 * blk, lev, m) for lev in range(2)]
            pack_store(zs, z, i + 8 * blk, lane)

        sender.send(8 * blk, 8)
    sender.wait()


ANY = pl.BlockSpec(memory_space=pl.ANY)
VM = pl.BlockSpec(memory_space=pltpu.VMEM)


def us(t):
    return pl.CostEstimate(
        flops=int(t * 1.1e9), bytes_accessed=int(t * 3.4e6), transcendentals=0
    )


def piece(n):
    return jax.ShapeDtypeStruct((2, n, ML, 128), F32)


def forecast_call(kernel, name, segments, n, count, outs, extra_out, args, cost):
    loaded = sum(length for _, length in segments)
    kept = (count, 2, ML, 512)
    return pl.pallas_call(
        kernel,
        out_shape=outs + extra_out,
        in_specs=[ANY] + [VM] * (len(args) - 1),
        out_specs=[ANY] * len(outs) + [VM] * len(extra_out),
        scratch_shapes=[
            pltpu.VMEM((4, ML, 2 * loaded + 8, 128), F32),
            pltpu.VMEM((4, 2, n, ML, 128), F32),
            pltpu.VMEM((64, 4, 8, 128), F32),
            pltpu.VMEM(kept, F32),
            pltpu.VMEM(kept, F32),
            pltpu.SemaphoreType.DMA((2, 4 * len(segments))),
            pltpu.SemaphoreType.DMA((n // 8 * len(outs),)),
        ],
        compiler_params=params(),
        cost_estimate=us(cost),
        name=name,
    )(*args)


def forecast_first(*args):
    n = ROWS_A[1]
    halo = pltpu.VMEM((72, 512), F32)
    return forecast_call(
        first_rows_kernel, "forecast_first", SEG_A, n, n + 4, [piece(n)] * 4, [halo, halo], args, 5
    )


def forecast_inner(*args):
    n = ROWS_B[1]
    return forecast_call(
        inner_rows_kernel, "forecast_inner", SEG_B, n, n + 4, [piece(n)] * 4, [], args, 9
    )


def forecast_edge(*args):
    return forecast_call(
        edge_rows_kernel,
        "forecast_edge",
        SEG_C,
        NE,
        24,
        [piece(NE)] * 4,
        [],
        args,
        0.1,
    )


def dot_nt(a, b):
    return lax.dot_general(a, b, (((1,), (1,)), ((), ())), preferred_element_type=F32)


def weight_kernel(count, cell, value, var, land, out, sea_out):
    me = lax.axis_index("mem")
    odd = me & 1
    slots = cell.shape[2]
    rows64 = lax.broadcasted_iota(jnp.int32, (64, slots), 0)
    rows128 = lax.broadcasted_iota(jnp.int32, (128, slots), 0)
    slot = lax.broadcasted_iota(jnp.int32, (1, slots), 1)
    sea = land[:, pl.ds(pl.multiple_of(me * 128, 128), 128)].astype(F32)
    lane = lax.broadcasted_iota(jnp.int32, (64, 128), 1)
    turned = pltpu.roll(sea, 64, 1)
    seas = (jnp.where(lane < 64, sea, turned), jnp.where(lane < 64, turned, sea))
    for b in range(2):
        c = cell[0, b : b + 1, :]
        live = slot < count[0, b]
        w = jnp.where(live, 1.0 / var[0, b : b + 1, :], 0.0)
        u = w * value[0, b : b + 1, :]
        at_row = rows64 == ((c >> 6) & 63)
        at_lane = rows128 == (((c >> 12) << 6) | (c & 63))
        terms = []
        for v in (w, u):
            hi = v.astype(BF16).astype(F32)
            terms += [jnp.where(at_row, t, 0.0).astype(BF16) for t in (hi, v - hi)]
        lhs = jnp.concatenate(terms, axis=0)
        rhs = jnp.where(at_lane, 1.0, 0.0).astype(BF16)
        full = dot_nt(lhs, rhs)
        fs = b ^ odd
        for n in range(2):
            v = (full[128 * n : 128 * n + 64] + full[128 * n + 64 : 128 * n + 128]) * seas[b]
            out[fs, n, 0:48] = v[8:56]
            out[fs, n, 48:56] = v[0:8]
            out[fs, n, 56:64] = v[56:64]
        sea_out[b] = seas[b]


def cell_weights(count, cell, value, var, land):
    return pl.pallas_call(
        weight_kernel,
        out_shape=[
            jax.ShapeDtypeStruct((2, 2, 64, 128), F32),
            jax.ShapeDtypeStruct((2, 64, 128), F32),
        ],
        in_specs=[pl.BlockSpec(memory_space=pltpu.SMEM), VM, VM, VM, VM],
        out_specs=[VM, VM],
        compiler_params=params(),
        cost_estimate=us(0.1),
        name="cell_weights",
    )(count, cell, value, var, land)


def gauss(off):
    return jnp.exp(-(off * off) / (2.0 * LOC * LOC))


GR = 208


def gram_rows(pieces, s_out, mean_out, wu, rows, acc, fs, lh, rh, rl, xo, me, begin=None):
    for k in range(4):
        at = pl.multiple_of((me ^ k) * ML, ML)
        xo[:, pl.ds(at, ML), :] = pieces[k][0]
    sub = lax.broadcasted_iota(jnp.int32, (8, 128), 0)
    c = (lax.broadcasted_iota(jnp.int32, (1, 128), 1) & 63).astype(F32)
    ec = [gauss(c - 31.5 - 64.0 * j) for j in (-1, 0, 1)]
    sub16 = lax.broadcasted_iota(jnp.int32, (16, 128), 0)
    for half in range(len(rows)):
        r = (sub + rows[half]).astype(F32)
        er = [gauss(r - 31.5 - 64.0 * i) for i in (-1, 0, 1)]
        w = wu[0, 0, 8 * half : 8 * half + 8, :]
        u = wu[0, 1, 8 * half : 8 * half + 8, :]
        wi = [w * e for e in er]
        ui = [u * e for e in er]
        for j8 in range(8):
            rr = 8 * half + j8
            x = xo[rr]
            mean = jnp.sum(x, axis=0, keepdims=True) * (1.0 / 64.0)
            mean_out[0, rr : rr + 1, :] = mean
            s = x - mean
            s_out[0, rr] = s
            cols = pl.ds(128 * rr, 128)
            drives = jnp.zeros((16, 128), F32)
            for i in range(3):
                wrow = wi[i][j8 : j8 + 1]
                hi, lo = two_terms(s * wrow)
                lh[pl.ds(64 * i, 64), cols] = hi
                lh[pl.ds(GR + 64 * i, 64), cols] = lo
                drives = jnp.where(sub16 == i, ui[i][j8 : j8 + 1] - wrow * mean, drives)
            hi, lo = two_terms(drives)
            lh[pl.ds(192, 16), cols] = hi
            lh[pl.ds(GR + 192, 16), cols] = lo
            for j in range(3):
                hi, lo = two_terms(s * ec[j])
                rh[pl.ds(64 * j, 64), cols] = hi
                rl[pl.ds(64 * j, 64), cols] = lo
    if begin is not None:
        begin()
    both = dot_nt(lh[...], rh[...])
    acc[fs] += both[0:GR] + both[GR : 2 * GR] + dot_nt(lh[0:GR, :], rl[...])


def gram_kernel(halves, groups, rows, stage, *refs):
    me = lax.axis_index("mem")
    g = pl.program_id(0)
    refs = list(refs)
    pieces = [refs.pop(0) for _ in range(4)]
    wu = refs.pop(0)
    acc_in = None
    if stage != "first":
        acc_in = refs.pop(0)
        del refs[0:2]
    acc, s_out, mean_out = (refs.pop(0) for _ in range(3))
    tmp = refs

    @pl.when(g == 0)
    def _():
        acc[...] = jnp.zeros_like(acc) if acc_in is None else acc_in[...]

    if len(halves) == 2:
        fs = g // groups
    else:
        fs = halves[0]
    first = [r + 16 * (g % groups) for r in rows]
    gram_rows(pieces, s_out, mean_out, wu, first, acc, fs, *tmp, me)


def near(x):
    return pltpu.with_memory_space_constraint(x, pltpu.VMEM)


def end_kernel(fs, *refs):
    me = lax.axis_index("mem")
    odd = (me & 1) == 1
    refs = list(refs)
    pieces = [refs.pop(0).at[pl.ds(fs, 1)] for _ in range(4)]
    wu = refs.pop(0).at[pl.ds(fs, 1), :, pl.ds(48, 16)]
    acc_in = refs.pop(0)
    del refs[0:2]
    spread, mean = refs.pop(0), refs.pop(0)
    extra = [refs.pop(0) for _ in range(2)]
    acc = refs.pop(0) if fs == 1 else extra[1]
    s_out, mean_out, sems = (refs.pop(0) for _ in range(3))
    acc[...] = acc_in[...]
    copies = [
        pltpu.make_async_copy(
            s_out, spread.at[pl.ds(fs, 1), pl.ds(48, 16)], sems.at[0]
        ),
        pltpu.make_async_copy(
            mean_out, mean.at[pl.ds(fs, 1), pl.ds(48, 16)], sems.at[1]
        ),
    ]

    def begin():
        for c in copies:
            c.start()

    gram_rows(pieces, s_out, mean_out, wu, (0, 56), acc, fs, *refs, me, begin)
    if fs == 0:
        d = acc[0]
        extra[0][...] = jnp.where(odd, d[:, 128:192], d[:, 0:64])
    else:
        b0 = acc[me & 1]
        b1 = acc[1 - (me & 1)]
        extra[0][...] = jnp.concatenate(
            [b0[:, 64:128] + b1[:, 0:64], b0[:, 128:192] + b1[:, 64:128]], axis=1
        )
        extra[1][...] = jnp.where(odd, b0[:, 0:64], b1[:, 128:192])
    for c in copies:
        c.wait()


def end_call(fs, pieces, wu, held, cost):
    acc, spread, mean = held
    if fs == 0:
        extra = [pltpu.VMEM((GR, 64), F32), pltpu.VMEM(acc.shape, F32)]
    else:
        extra = [pltpu.VMEM((GR, 128), F32), pltpu.VMEM((GR, 64), F32)]
    args = [near(p) for p in pieces] + [near(wu), near(acc), spread, mean]
    return pl.pallas_call(
        functools.partial(end_kernel, fs),
        out_shape=[
            jax.ShapeDtypeStruct(spread.shape, F32),
            jax.ShapeDtypeStruct(mean.shape, F32),
        ]
        + extra,
        in_specs=[VM] * 6 + [ANY] * 2,
        out_specs=[ANY, ANY, VM, VM],
        input_output_aliases={6: 0, 7: 1},
        scratch_shapes=[pltpu.VMEM(acc.shape, F32)] * fs
        + [
            pltpu.VMEM((1, 16, 64, 128), F32),
            pltpu.VMEM((1, 16, 128), F32),
            pltpu.SemaphoreType.DMA((2,)),
            pltpu.VMEM((2 * GR, 2048), BF16),
            pltpu.VMEM((192, 2048), BF16),
            pltpu.VMEM((192, 2048), BF16),
            pltpu.VMEM((16, 64, 128), F32),
        ],
        compiler_params=params(),
        cost_estimate=us(cost),
        name=("gram_border", "gram_last")[fs],
    )(*args)


def WHOLE(shape):
    return pl.BlockSpec(shape, lambda g: (0,) * len(shape))


def gram_call(stage, halves, groups, kept, rows, pieces, wu, held, cost):
    n = 16
    fs_of = (lambda g: g // groups) if len(halves) == 2 else (lambda g: halves[0])
    sub = lambda g: g % groups
    ins = [pl.BlockSpec((1, n, ML, 128), lambda g: (fs_of(g), sub(g), 0, 0))] * 4
    ins.append(pl.BlockSpec((1, 2, n, 128), lambda g: (fs_of(g), 0, kept + sub(g), 0)))
    args = list(pieces) + [wu]
    acc_shape = (2, GR, 192)
    outs = [
        pltpu.VMEM(acc_shape, F32),
        jax.ShapeDtypeStruct((2, BS, 64, 128), F32),
        jax.ShapeDtypeStruct((2, BS, 128), F32),
    ]
    out_specs = [
        WHOLE(acc_shape),
        pl.BlockSpec((1, n, 64, 128), lambda g: (fs_of(g), kept + sub(g), 0, 0)),
        pl.BlockSpec((1, n, 128), lambda g: (fs_of(g), kept + sub(g), 0)),
    ]
    aliases = {}
    if stage != "first":
        aliases = {len(args) + 1: 1, len(args) + 2: 2}
        ins += [WHOLE(acc_shape)] + [pl.BlockSpec(memory_space=pl.ANY)] * 2
        args += list(held)
    return pl.pallas_call(
        functools.partial(gram_kernel, halves, groups, rows, stage),
        grid=(len(halves) * groups,),
        out_shape=outs,
        in_specs=ins,
        out_specs=out_specs,
        input_output_aliases=aliases,
        scratch_shapes=[
            pltpu.VMEM((2 * GR, 128 * n), BF16),
            pltpu.VMEM((192, 128 * n), BF16),
            pltpu.VMEM((192, 128 * n), BF16),
            pltpu.VMEM((n, 64, 128), F32),
        ],
        compiler_params=params(),
        cost_estimate=us(cost),
        name="gram_" + stage,
    )(*args)


def join_kernel(mid, core, border, down, own, up):
    odd = (lax.axis_index("mem") & 1) == 1
    c = core[...]
    b = border[...]
    q = mid[...] + jnp.concatenate([jnp.where(odd, c, b), jnp.where(odd, b, c)], axis=1)
    for i, ref in enumerate((down, own, up)):
        ref[0:64] = q[64 * i : 64 * i + 64]
        ref[64:72] = jnp.broadcast_to(q[192 + i : 193 + i], (8, 128))


def join(mid, core, border):
    one = pltpu.VMEM((72, 128), F32)
    mid, core, border = near(mid), near(core), near(border)
    return pl.pallas_call(
        join_kernel,
        out_shape=[one, one, one],
        in_specs=[VM, VM, VM],
        out_specs=[VM, VM, VM],
        compiler_params=params(),
        cost_estimate=us(0.1),
        name="join_grams",
    )(mid, core, border)


def dot32(a, b):
    return lax.dot_general(
        a, b, (((1,), (0,)), ((), ())), precision=HIGHEST, preferred_element_type=F32
    )


def weights_of(gram, drive):
    n = gram.shape[0]
    eye = (
        lax.broadcasted_iota(jnp.int32, (n, n), 0) == lax.broadcasted_iota(jnp.int32, (n, n), 1)
    ).astype(F32)
    system = (n - 1.0) * eye + gram
    squares = jnp.sum(jnp.sum(system * system, axis=1, keepdims=True), axis=0, keepdims=True)
    frob = jnp.sqrt(squares)
    iterate = system / frob
    root = None
    for it in range(NSI):
        prod = iterate if root is None else dot32(root, iterate)
        corr = 1.5 * eye - 0.5 * prod
        if it < NSI - 1:
            iterate = dot32(iterate, corr)
        root = corr if root is None else dot32(corr, root)
    half = root / jnp.sqrt(frob)
    row = dot32(dot32(jnp.broadcast_to(drive, (8, n)), half), half)
    return jnp.sqrt(n - 1.0) * half + row[0:1]


YS = 68


def kept_at(n):
    return jnp.where(n == 0, 6, jnp.where(n == 7, 7, n - 1)) * 8


def analysis_kernel(
    own, fromlow, fromhigh, mean, sea, spread, out, sv, tt, rhs, ys, ov, isem, osem
):
    me = lax.axis_index("mem")
    odd = me & 1

    def fetch(n):
        rows = pl.ds(pl.multiple_of(kept_at(n), 8), 8)
        return pltpu.make_async_copy(spread.at[:, rows], sv.at[n], isem.at[n])

    def store(half, n):
        rows = pl.ds(pl.multiple_of(8 * n, 8), 8)
        return pltpu.make_async_copy(ov.at[half], out.at[:, :, rows], osem.at[half])

    for n in range(8):
        fetch(jnp.int32(n)).start()
    tot = own[...] + fromlow[...] + fromhigh[...]
    for b in range(2):
        t = tot[:, 64 * b : 64 * b + 64]
        hi, lo = two_terms(weights_of(t[0:64], t[64:65]))
        tt[b] = jnp.concatenate([hi, hi, lo], axis=1)
    lane = lax.broadcasted_iota(jnp.int32, (64, 128), 1)

    @pl.loop(0, 4)
    def _(i):
        for half in range(2):
            n = 2 * i + half
            fetch(n).wait()
            upd = []
            for b in range(2):
                for rr in range(8):
                    hi, lo = two_terms(sv[n, b ^ odd, rr])
                    cols = pl.ds(128 * rr, 128)
                    rhs[half, b, 0:64, cols] = hi
                    rhs[half, b, 64:128, cols] = lo
                    rhs[half, b, 128:192, cols] = hi
                upd.append(
                    lax.dot_general(
                        tt[b], rhs[half, b], (((1,), (0,)), ((), ())), preferred_element_type=F32
                    )
                )
            m8 = [
                mean[b ^ odd, pl.ds(pl.multiple_of(kept_at(n), 8), 8), :] for b in range(2)
            ]
            sea8 = [sea[b, pl.ds(pl.multiple_of(8 * n, 8), 8), :] for b in range(2)]
            for rr in range(8):
                res = []
                for b in range(2):
                    x = sv[n, b ^ odd, rr]
                    up = upd[b][:, 128 * rr : 128 * rr + 128]
                    res.append((m8[b][rr : rr + 1] + x) + sea8[b][rr : rr + 1] * (up - x))
                at = pl.ds(YS * rr, 64)
                ys[half, 0, at, :] = jnp.where(lane < 64, res[0], pltpu.roll(res[1], 64, 1))
                ys[half, 1, at, :] = jnp.where(lane < 64, pltpu.roll(res[0], 64, 1), res[1])

            @pl.when(i > 0)
            def _(half=half, n=n):
                store(half, n).wait()

            for m in range(64):
                for lev in range(2):
                    ov[half, m, lev] = ys[half, lev, pl.ds(m, 8, stride=YS), :]
            store(half, n).start()

    for half in range(2):
        store(half, jnp.int32(6 + half)).wait()


def analysis(own, fromlow, fromhigh, s, mean, sea):
    return pl.pallas_call(
        analysis_kernel,
        out_shape=jax.ShapeDtypeStruct((64, 2, 64, 128), F32),
        in_specs=[VM] * 5 + [ANY],
        out_specs=ANY,
        scratch_shapes=[
            pltpu.VMEM((8, 2, 8, 64, 128), F32),
            pltpu.VMEM((2, 64, 192), BF16),
            pltpu.VMEM((2, 2, 192, 1024), BF16),
            pltpu.VMEM((2, 2, 8 * YS, 128), F32),
            pltpu.VMEM((2, 64, 2, 8, 128), F32),
            pltpu.SemaphoreType.DMA((8,)),
            pltpu.SemaphoreType.DMA((2,)),
        ],
        compiler_params=params(),
        cost_estimate=us(8),
        name="analysis",
    )(near(own), near(fromlow), near(fromhigh), mean, sea, s)


def per_device(state, diffusivity, land_sea, obs_value, obs_var, obs_cell, obs_count):
    tiles = lax.axis_size("tile")
    up = [(i, i + 1) for i in range(tiles - 1)]
    down = [(i + 1, i) for i in range(tiles - 1)]
    swap = lambda k: [(i, i ^ k) for i in range(4)]

    mem = lambda v, k: lax.ppermute(v, "mem", swap(k))
    after = lax.optimization_barrier

    a = list(forecast_first(state, diffusivity, land_sea))
    a2, a3, a1 = mem(a[2], 2), mem(a[3], 3), mem(a[1], 1)
    hup, hdn, a1 = after((a[4], a[5], a1))
    above = lax.ppermute(hup, "tile", up)
    below = lax.ppermute(hdn, "tile", down)
    a[0], land_b = after((a[0], land_sea))
    b = list(forecast_inner(state, diffusivity, land_b))
    b2, b3, b1 = mem(b[2], 2), mem(b[3], 3), mem(b[1], 1)
    land_e, b[0] = after((land_sea, b[0]))
    e = list(forecast_edge(state, diffusivity, land_e, near(above), near(below)))
    e2, e3, e1 = mem(e[2], 2), mem(e[3], 3), mem(e[1], 1)
    obs_cell, e1 = after((obs_cell, e1))
    wu, sea = cell_weights(obs_count, obs_cell, obs_value, obs_var, land_sea)
    held = gram_call("first", (0, 1), 2, 1, (24, 32), (a[0], a1, a2, a3), wu, None, 0.1)
    held = gram_call("inner", (0, 1), 1, 0, (8, 16), (b[0], b1, b2, b3), wu, held, 0.1)
    edge = (e[0], e1, e2, e3)
    s, mean, border, acc = end_call(0, edge, wu, held, 3)
    border = lax.ppermute(border, "mem", [(1, 2), (2, 1)])
    s, mean, mid, core = end_call(1, edge, wu, (acc, s, mean), 4)
    core, border = after((core, border))
    core = mem(core, 1)
    to_low, own, to_high = join(mid, core, border)
    fromlow = lax.ppermute(to_high, "tile", up)
    fromhigh = lax.ppermute(to_low, "tile", down)
    return analysis(own, fromlow, fromhigh, s, mean, sea)


def solution(mesh):
    return jax.shard_map(
        per_device,
        mesh=mesh,
        in_specs=(
            P("mem", None, "tile", None),
            P("tile", None),
            P("tile", None),
            P("tile", "mem", None),
            P("tile", "mem", None),
            P("tile", "mem", None),
            P("tile", "mem"),
        ),
        out_specs=P(None, None, "tile", "mem"),
        check_vma=False,
    )
```

```python
import functools

import jax
import jax.numpy as jnp
from jax import lax
from jax.experimental import pallas as pl
from jax.experimental.pallas import tpu as pltpu
from jax.sharding import PartitionSpec as P

NSI = 4
LOC = 48.0
BS = 64
UNROLL = 4
UNROLL_B = 6
ML = 16
NE = 16
F32 = jnp.float32
BF16 = jnp.bfloat16
VMEM_LIMIT = 56 * 1024 * 1024
HIGHEST = lax.Precision.HIGHEST


def params(**kw):
    return pltpu.CompilerParams(vmem_limit_bytes=VMEM_LIMIT, **kw)


def two_terms(x):
    hi = x.astype(BF16)
    lo = (x - hi.astype(F32)).astype(BF16)
    return hi, lo


def pack_store(zs, z, row, lane):
    low = lane < 64
    for q in range(4):
        r0 = pltpu.roll(z[0][q], 64, 1)
        r1 = pltpu.roll(z[1][q], 64, 1)
        pair = (jnp.where(low, z[0][q], r1), jnp.where(low, r0, z[1][q]))
        for b in range(2):
            zs[q, b ^ (q & 1), row] = pair[b]


def fill_md(md, dif, land, rows):
    for r8 in sorted({r // 8 for r in rows}):
        m = land[8 * r8 : 8 * r8 + 8, :].astype(F32) * dif[8 * r8 : 8 * r8 + 8, :]
        for j in range(8):
            if 8 * r8 + j in rows:
                for q in range(4):
                    md[8 * r8 + j, q] = jnp.broadcast_to(
                        m[j : j + 1, 128 * q : 128 * q + 128], (8, 128)
                    )


def md_row(md, r):
    return [jnp.concatenate([md[r, q], md[r, q]], axis=0) for q in range(4)]


class Rows:
    def __init__(self, state, xs, sems, segments):
        self.n = sum(length for _, length in segments)
        self.stride = 2 * self.n + 8
        self.flat = xs.reshape(4 * ML * self.stride, 128)
        self.segments = segments
        self.copies = {}
        for lev in range(2):
            at = 0
            for i, (start, length) in enumerate(segments):
                self.copies[lev, i] = [
                    pltpu.make_async_copy(
                        state.at[:, lev, pl.ds(start, length), pl.ds(128 * q, 128)],
                        xs.at[q, :, pl.ds(lev * self.n + at, length)],
                        sems.at[lev, i * 4 + q],
                    )
                    for q in range(4)
                ]
                at += length

    def start(self, order=None):
        for i in order or range(len(self.segments)):
            for lev in range(2):
                for c in self.copies[lev, i]:
                    c.start()

    def wait(self, lev, which=None):
        for i in which or range(len(self.segments)):
            for c in self.copies[lev, i]:
                c.wait()

    def offset(self, r):
        at = 0
        for start, length in self.segments:
            if start <= r < start + length:
                return r - start + at
            at += length
        raise ValueError(r)

    def load(self, lev, off):
        return [
            self.flat[pl.ds(q * ML * self.stride + lev * self.n + off, ML, stride=self.stride), :]
            for q in range(4)
        ]


class Stencil:
    def __init__(self, x, y):
        self.x = x
        self.y = y
        self.lane = lax.broadcasted_iota(jnp.int32, (ML, 128), 1)

    def put(self, ref, p, lev, tiles):
        for q in range(4):
            ref[p, lev, :, pl.ds(128 * q, 128)] = tiles[q]

    def step(self, ref, p, lev, md):
        mid = [ref[p, lev, :, pl.ds(128 * q, 128)] for q in range(4)]
        fwd = [pltpu.roll(t, 1, 1) for t in mid]
        bwd = [pltpu.roll(t, 127, 1) for t in mid]
        zero = jnp.zeros_like(mid[0])
        out = []
        for q in range(4):
            cols = pl.ds(128 * q, 128)
            left = jnp.where(self.lane == 0, fwd[q - 1] if q > 0 else zero, fwd[q])
            right = jnp.where(self.lane == 127, bwd[q + 1] if q < 3 else zero, bwd[q])
            near = (ref[p - 1, lev, :, cols] + ref[p + 1, lev, :, cols]) + (left + right)
            out.append(mid[q] + md[q] * (near - 4.0 * mid[q]))
        return out


class Sender:
    def __init__(self, zs, outs, me, sems):
        self.zs = zs
        self.outs = outs
        self.me = me
        self.sems = sems
        self.copies = []

    def send(self, at, length):
        for k in range(4):
            c = pltpu.make_async_copy(
                self.zs.at[self.me ^ k, :, pl.ds(at, length)],
                self.outs[k].at[:, pl.ds(at, length)],
                self.sems.at[len(self.copies)],
            )
            c.start()
            self.copies.append(c)

    def wait(self):
        for c in self.copies:
            c.wait()


SEG_A = ((16, 24), (40, 24), (0, 8))
SEG_B = ((0, 32),)
SEG_C = ((0, 16), (48, 16))
ROWS_A = (24, 32)
ROWS_B = (8, 16)


def plain_rows(rows, st, md, zs, sender, r0, n, parts):
    off = rows.offset(r0 - 2)
    lane = lax.broadcasted_iota(jnp.int32, (ML, 128), 1)
    low, made = 0, 1
    for segment, high in parts:
        for lev in range(2):
            rows.wait(lev, (segment,))

            @pl.loop(low, high, unroll=2)
            def _(p, lev=lev):
                st.put(st.x, p, lev, rows.load(lev, off + p))

        @pl.loop(made, high - 1, unroll=UNROLL_B)
        def _(p):
            m = md_row(md, p + (r0 - 2))
            for lev in range(2):
                st.put(st.y, p, lev, st.step(st.x, p, lev, m))

        low, made = high, high - 1

    for blk in range(n // 8):

        @pl.loop(8 * blk, 8 * blk + 8, unroll=UNROLL)
        def _(i):
            m = md_row(md, i + r0)
            pack_store(zs, [st.step(st.y, i + 2, lev, m) for lev in range(2)], i, lane)

        sender.send(8 * blk, 8)
    sender.wait()


def first_rows_kernel(
    state, dif, land, o0, o1, o2, o3, hup, hdn, xs, zs, md, x, y, isem, osem
):
    rows = Rows(state, xs, isem, SEG_A)
    rows.start()
    r0, n = ROWS_A
    fill_md(md, dif, land, [0, 63, *range(r0 - 1, r0 + n + 1)])
    st = Stencil(x, y)
    sender = Sender(zs, (o0, o1, o2, o3), lax.axis_index("mem"), osem)
    plain_rows(rows, st, md, zs, sender, r0, n, ((0, 18), (1, 36)))
    for lev in range(2):
        rows.wait(lev, (2,))
    for j in range(2):
        for lev in range(2):
            for ref, r in ((hdn, j), (hup, 62 + j)):
                v = rows.load(lev, rows.offset(r))
                for q in range(4):
                    ref[pl.ds(j * 32 + lev * 16, 16), pl.ds(128 * q, 128)] = v[q]
    for ref, r in ((hup, 63), (hdn, 0)):
        for q in range(4):
            ref[64:72, 128 * q : 128 * q + 128] = md[r, q]


def inner_rows_kernel(
    state, dif, land, o0, o1, o2, o3, xs, zs, md, x, y, isem, osem
):
    rows = Rows(state, xs, isem, SEG_B)
    rows.start()
    r0, n = ROWS_B
    fill_md(md, dif, land, range(r0 - 1, r0 + n + 1))
    st = Stencil(x, y)
    sender = Sender(zs, (o0, o1, o2, o3), lax.axis_index("mem"), osem)
    plain_rows(rows, st, md, zs, sender, r0, n, ((0, n + 4),))


def edge_rows_kernel(
    state, dif, land, above, below, o0, o1, o2, o3, xs, zs, md, x, y, isem, osem
):
    rows = Rows(state, xs, isem, SEG_C)
    rows.start()
    fill_md(md, dif, land, [*range(9), *range(55, 64)])
    st = Stencil(x, y)
    sender = Sender(zs, (o0, o1, o2, o3), lax.axis_index("mem"), osem)
    lane = lax.broadcasted_iota(jnp.int32, (ML, 128), 1)
    for ref, p0 in ((above, 0), (below, 22)):
        for j in range(2):
            for lev in range(2):
                at = pl.ds(j * 32 + lev * 16, 16)
                st.put(x, p0 + j, lev, [ref[at, 128 * q : 128 * q + 128] for q in range(4)])
    for lev in range(2):
        rows.wait(lev)

        @pl.loop(0, 10, unroll=2)
        def _(i, lev=lev):
            st.put(x, i + 2, lev, rows.load(lev, i))
            st.put(x, i + 12, lev, rows.load(lev, i + 22))

    def outside(ref):
        tiles = [ref[64:72, 128 * q : 128 * q + 128] for q in range(4)]
        return [jnp.concatenate([t, t], axis=0) for t in tiles]

    for p, ref in ((1, above), (22, below)):
        for lev in range(2):
            st.put(y, p, lev, st.step(x, p, lev, outside(ref)))

    @pl.loop(0, 9, unroll=3)
    def _(i):
        m = md_row(md, i)
        w = md_row(md, i + 55)
        for lev in range(2):
            st.put(y, i + 2, lev, st.step(x, i + 2, lev, m))
            st.put(y, i + 13, lev, st.step(x, i + 13, lev, w))

    for blk in range(2):

        @pl.loop(0, 8, unroll=UNROLL)
        def _(i, blk=blk):
            m = md_row(md, i + 56 * blk)
            z = [st.step(y, i + 2 + 12 * blk, lev, m) for lev in range(2)]
            pack_store(zs, z, i + 8 * blk, lane)

        sender.send(8 * blk, 8)
    sender.wait()


ANY = pl.BlockSpec(memory_space=pl.ANY)
VM = pl.BlockSpec(memory_space=pltpu.VMEM)


def us(t):
    return pl.CostEstimate(
        flops=int(t * 1.1e9), bytes_accessed=int(t * 3.4e6), transcendentals=0
    )


def piece(n):
    return jax.ShapeDtypeStruct((2, n, ML, 128), F32)


def forecast_call(kernel, name, segments, n, count, outs, extra_out, args, cost):
    loaded = sum(length for _, length in segments)
    kept = (count, 2, ML, 512)
    return pl.pallas_call(
        kernel,
        out_shape=outs + extra_out,
        in_specs=[ANY] + [VM] * (len(args) - 1),
        out_specs=[ANY] * len(outs) + [VM] * len(extra_out),
        scratch_shapes=[
            pltpu.VMEM((4, ML, 2 * loaded + 8, 128), F32),
            pltpu.VMEM((4, 2, n, ML, 128), F32),
            pltpu.VMEM((64, 4, 8, 128), F32),
            pltpu.VMEM(kept, F32),
            pltpu.VMEM(kept, F32),
            pltpu.SemaphoreType.DMA((2, 4 * len(segments))),
            pltpu.SemaphoreType.DMA((n // 8 * len(outs),)),
        ],
        compiler_params=params(),
        cost_estimate=us(cost),
        name=name,
    )(*args)


def forecast_first(*args):
    n = ROWS_A[1]
    halo = pltpu.VMEM((72, 512), F32)
    return forecast_call(
        first_rows_kernel, "forecast_first", SEG_A, n, n + 4, [piece(n)] * 4, [halo, halo], args, 5
    )


def forecast_inner(*args):
    n = ROWS_B[1]
    return forecast_call(
        inner_rows_kernel, "forecast_inner", SEG_B, n, n + 4, [piece(n)] * 4, [], args, 9
    )


def forecast_edge(*args):
    return forecast_call(
        edge_rows_kernel,
        "forecast_edge",
        SEG_C,
        NE,
        24,
        [piece(NE)] * 4,
        [],
        args,
        0.1,
    )


def dot_nt(a, b):
    return lax.dot_general(a, b, (((1,), (1,)), ((), ())), preferred_element_type=F32)


def weight_kernel(count, cell, value, var, land, out, sea_out):
    me = lax.axis_index("mem")
    odd = me & 1
    slots = cell.shape[2]
    rows64 = lax.broadcasted_iota(jnp.int32, (64, slots), 0)
    rows128 = lax.broadcasted_iota(jnp.int32, (128, slots), 0)
    slot = lax.broadcasted_iota(jnp.int32, (1, slots), 1)
    sea = land[:, pl.ds(pl.multiple_of(me * 128, 128), 128)].astype(F32)
    lane = lax.broadcasted_iota(jnp.int32, (64, 128), 1)
    turned = pltpu.roll(sea, 64, 1)
    seas = (jnp.where(lane < 64, sea, turned), jnp.where(lane < 64, turned, sea))
    for b in range(2):
        c = cell[0, b : b + 1, :]
        live = slot < count[0, b]
        w = jnp.where(live, 1.0 / var[0, b : b + 1, :], 0.0)
        u = w * value[0, b : b + 1, :]
        at_row = rows64 == ((c >> 6) & 63)
        at_lane = rows128 == (((c >> 12) << 6) | (c & 63))
        terms = []
        for v in (w, u):
            hi = v.astype(BF16).astype(F32)
            terms += [jnp.where(at_row, t, 0.0).astype(BF16) for t in (hi, v - hi)]
        lhs = jnp.concatenate(terms, axis=0)
        rhs = jnp.where(at_lane, 1.0, 0.0).astype(BF16)
        full = dot_nt(lhs, rhs)
        fs = b ^ odd
        for n in range(2):
            v = (full[128 * n : 128 * n + 64] + full[128 * n + 64 : 128 * n + 128]) * seas[b]
            out[fs, n, 0:48] = v[8:56]
            out[fs, n, 48:56] = v[0:8]
            out[fs, n, 56:64] = v[56:64]
        sea_out[b] = seas[b]


def cell_weights(count, cell, value, var, land):
    return pl.pallas_call(
        weight_kernel,
        out_shape=[
            jax.ShapeDtypeStruct((2, 2, 64, 128), F32),
            jax.ShapeDtypeStruct((2, 64, 128), F32),
        ],
        in_specs=[pl.BlockSpec(memory_space=pltpu.SMEM), VM, VM, VM, VM],
        out_specs=[VM, VM],
        compiler_params=params(),
        cost_estimate=us(0.1),
        name="cell_weights",
    )(count, cell, value, var, land)


def gauss(off):
    return jnp.exp(-(off * off) / (2.0 * LOC * LOC))


GR = 208


def gram_rows(pieces, s_out, mean_out, wu, rows, acc, fs, lh, rh, rl, xo, me, begin=None):
    for k in range(4):
        at = pl.multiple_of((me ^ k) * ML, ML)
        xo[:, pl.ds(at, ML), :] = pieces[k][0]
    sub = lax.broadcasted_iota(jnp.int32, (8, 128), 0)
    c = (lax.broadcasted_iota(jnp.int32, (1, 128), 1) & 63).astype(F32)
    ec = [gauss(c - 31.5 - 64.0 * j) for j in (-1, 0, 1)]
    sub16 = lax.broadcasted_iota(jnp.int32, (16, 128), 0)
    for half in range(len(rows)):
        r = (sub + rows[half]).astype(F32)
        er = [gauss(r - 31.5 - 64.0 * i) for i in (-1, 0, 1)]
        w = wu[0, 0, 8 * half : 8 * half + 8, :]
        u = wu[0, 1, 8 * half : 8 * half + 8, :]
        wi = [w * e for e in er]
        ui = [u * e for e in er]
        for j8 in range(8):
            rr = 8 * half + j8
            x = xo[rr]
            mean = jnp.sum(x, axis=0, keepdims=True) * (1.0 / 64.0)
            mean_out[0, rr : rr + 1, :] = mean
            s = x - mean
            s_out[0, rr] = s
            cols = pl.ds(128 * rr, 128)
            drives = jnp.zeros((16, 128), F32)
            for i in range(3):
                wrow = wi[i][j8 : j8 + 1]
                hi, lo = two_terms(s * wrow)
                lh[pl.ds(64 * i, 64), cols] = hi
                lh[pl.ds(GR + 64 * i, 64), cols] = lo
                drives = jnp.where(sub16 == i, ui[i][j8 : j8 + 1] - wrow * mean, drives)
            hi, lo = two_terms(drives)
            lh[pl.ds(192, 16), cols] = hi
            lh[pl.ds(GR + 192, 16), cols] = lo
            for j in range(3):
                hi, lo = two_terms(s * ec[j])
                rh[pl.ds(64 * j, 64), cols] = hi
                rl[pl.ds(64 * j, 64), cols] = lo
    if begin is not None:
        begin()
    both = dot_nt(lh[...], rh[...])
    acc[fs] += both[0:GR] + both[GR : 2 * GR] + dot_nt(lh[0:GR, :], rl[...])


def gram_kernel(halves, groups, rows, stage, *refs):
    me = lax.axis_index("mem")
    g = pl.program_id(0)
    refs = list(refs)
    pieces = [refs.pop(0) for _ in range(4)]
    wu = refs.pop(0)
    acc_in = None
    if stage != "first":
        acc_in = refs.pop(0)
        del refs[0:2]
    acc, s_out, mean_out = (refs.pop(0) for _ in range(3))
    tmp = refs

    @pl.when(g == 0)
    def _():
        acc[...] = jnp.zeros_like(acc) if acc_in is None else acc_in[...]

    if len(halves) == 2:
        fs = g // groups
    else:
        fs = halves[0]
    first = [r + 16 * (g % groups) for r in rows]
    gram_rows(pieces, s_out, mean_out, wu, first, acc, fs, *tmp, me)


def near(x):
    return pltpu.with_memory_space_constraint(x, pltpu.VMEM)


def end_kernel(fs, *refs):
    me = lax.axis_index("mem")
    odd = (me & 1) == 1
    refs = list(refs)
    pieces = [refs.pop(0).at[pl.ds(fs, 1)] for _ in range(4)]
    wu = refs.pop(0).at[pl.ds(fs, 1), :, pl.ds(48, 16)]
    acc_in = refs.pop(0)
    del refs[0:2]
    spread, mean = refs.pop(0), refs.pop(0)
    extra = [refs.pop(0) for _ in range(2)]
    acc = refs.pop(0) if fs == 1 else extra[1]
    s_out, mean_out, sems = (refs.pop(0) for _ in range(3))
    acc[...] = acc_in[...]
    copies = [
        pltpu.make_async_copy(
            s_out, spread.at[pl.ds(fs, 1), pl.ds(48, 16)], sems.at[0]
        ),
        pltpu.make_async_copy(
            mean_out, mean.at[pl.ds(fs, 1), pl.ds(48, 16)], sems.at[1]
        ),
    ]

    def begin():
        for c in copies:
            c.start()

    gram_rows(pieces, s_out, mean_out, wu, (0, 56), acc, fs, *refs, me, begin)
    if fs == 0:
        d = acc[0]
        extra[0][...] = jnp.where(odd, d[:, 128:192], d[:, 0:64])
    else:
        b0 = acc[me & 1]
        b1 = acc[1 - (me & 1)]
        extra[0][...] = jnp.concatenate(
            [b0[:, 64:128] + b1[:, 0:64], b0[:, 128:192] + b1[:, 64:128]], axis=1
        )
        extra[1][...] = jnp.where(odd, b0[:, 0:64], b1[:, 128:192])
    for c in copies:
        c.wait()


def end_call(fs, pieces, wu, held, cost):
    acc, spread, mean = held
    if fs == 0:
        extra = [pltpu.VMEM((GR, 64), F32), pltpu.VMEM(acc.shape, F32)]
    else:
        extra = [pltpu.VMEM((GR, 128), F32), pltpu.VMEM((GR, 64), F32)]
    args = [near(p) for p in pieces] + [near(wu), near(acc), spread, mean]
    return pl.pallas_call(
        functools.partial(end_kernel, fs),
        out_shape=[
            jax.ShapeDtypeStruct(spread.shape, F32),
            jax.ShapeDtypeStruct(mean.shape, F32),
        ]
        + extra,
        in_specs=[VM] * 6 + [ANY] * 2,
        out_specs=[ANY, ANY, VM, VM],
        input_output_aliases={6: 0, 7: 1},
        scratch_shapes=[pltpu.VMEM(acc.shape, F32)] * fs
        + [
            pltpu.VMEM((1, 16, 64, 128), F32),
            pltpu.VMEM((1, 16, 128), F32),
            pltpu.SemaphoreType.DMA((2,)),
            pltpu.VMEM((2 * GR, 2048), BF16),
            pltpu.VMEM((192, 2048), BF16),
            pltpu.VMEM((192, 2048), BF16),
            pltpu.VMEM((16, 64, 128), F32),
        ],
        compiler_params=params(),
        cost_estimate=us(cost),
        name=("gram_border", "gram_last")[fs],
    )(*args)


def WHOLE(shape):
    return pl.BlockSpec(shape, lambda g: (0,) * len(shape))


def gram_call(stage, halves, groups, kept, rows, pieces, wu, held, cost):
    n = 16
    fs_of = (lambda g: g // groups) if len(halves) == 2 else (lambda g: halves[0])
    sub = lambda g: g % groups
    ins = [pl.BlockSpec((1, n, ML, 128), lambda g: (fs_of(g), sub(g), 0, 0))] * 4
    ins.append(pl.BlockSpec((1, 2, n, 128), lambda g: (fs_of(g), 0, kept + sub(g), 0)))
    args = list(pieces) + [wu]
    acc_shape = (2, GR, 192)
    outs = [
        pltpu.VMEM(acc_shape, F32),
        jax.ShapeDtypeStruct((2, BS, 64, 128), F32),
        jax.ShapeDtypeStruct((2, BS, 128), F32),
    ]
    out_specs = [
        WHOLE(acc_shape),
        pl.BlockSpec((1, n, 64, 128), lambda g: (fs_of(g), kept + sub(g), 0, 0)),
        pl.BlockSpec((1, n, 128), lambda g: (fs_of(g), kept + sub(g), 0)),
    ]
    aliases = {}
    if stage != "first":
        aliases = {len(args) + 1: 1, len(args) + 2: 2}
        ins += [WHOLE(acc_shape)] + [pl.BlockSpec(memory_space=pl.ANY)] * 2
        args += list(held)
    return pl.pallas_call(
        functools.partial(gram_kernel, halves, groups, rows, stage),
        grid=(len(halves) * groups,),
        out_shape=outs,
        in_specs=ins,
        out_specs=out_specs,
        input_output_aliases=aliases,
        scratch_shapes=[
            pltpu.VMEM((2 * GR, 128 * n), BF16),
            pltpu.VMEM((192, 128 * n), BF16),
            pltpu.VMEM((192, 128 * n), BF16),
            pltpu.VMEM((n, 64, 128), F32),
        ],
        compiler_params=params(),
        cost_estimate=us(cost),
        name="gram_" + stage,
    )(*args)


def join_kernel(mid, core, border, down, own, up):
    odd = (lax.axis_index("mem") & 1) == 1
    c = core[...]
    b = border[...]
    q = mid[...] + jnp.concatenate([jnp.where(odd, c, b), jnp.where(odd, b, c)], axis=1)
    for i, ref in enumerate((down, own, up)):
        ref[0:64] = q[64 * i : 64 * i + 64]
        ref[64:72] = jnp.broadcast_to(q[192 + i : 193 + i], (8, 128))


def join(mid, core, border):
    one = pltpu.VMEM((72, 128), F32)
    mid, core, border = near(mid), near(core), near(border)
    return pl.pallas_call(
        join_kernel,
        out_shape=[one, one, one],
        in_specs=[VM, VM, VM],
        out_specs=[VM, VM, VM],
        compiler_params=params(),
        cost_estimate=us(0.1),
        name="join_grams",
    )(mid, core, border)


def dot32(a, b):
    return lax.dot_general(
        a, b, (((1,), (0,)), ((), ())), precision=HIGHEST, preferred_element_type=F32
    )


def weights_of(gram, drive):
    n = gram.shape[0]
    eye = (
        lax.broadcasted_iota(jnp.int32, (n, n), 0) == lax.broadcasted_iota(jnp.int32, (n, n), 1)
    ).astype(F32)
    system = (n - 1.0) * eye + gram
    squares = jnp.sum(jnp.sum(system * system, axis=1, keepdims=True), axis=0, keepdims=True)
    frob = jnp.sqrt(squares)
    iterate = system / frob
    root = None
    for it in range(NSI):
        prod = iterate if root is None else dot32(root, iterate)
        corr = 1.5 * eye - 0.5 * prod
        if it < NSI - 1:
            iterate = dot32(iterate, corr)
        root = corr if root is None else dot32(corr, root)
    half = root / jnp.sqrt(frob)
    row = dot32(dot32(jnp.broadcast_to(drive, (8, n)), half), half)
    return jnp.sqrt(n - 1.0) * half + row[0:1]


YS = 68


def kept_at(n):
    return jnp.where(n == 0, 6, jnp.where(n == 7, 7, n - 1)) * 8


def analysis_kernel(
    own, fromlow, fromhigh, mean, sea, spread, out, sv, tt, rhs, ys, ov, isem, osem
):
    me = lax.axis_index("mem")
    odd = me & 1

    def fetch(n):
        rows = pl.ds(pl.multiple_of(kept_at(n), 8), 8)
        return pltpu.make_async_copy(spread.at[:, rows], sv.at[n], isem.at[n])

    def store(half, n):
        rows = pl.ds(pl.multiple_of(8 * n, 8), 8)
        return pltpu.make_async_copy(ov.at[half], out.at[:, :, rows], osem.at[half])

    for n in range(8):
        fetch(jnp.int32(n)).start()
    tot = own[...] + fromlow[...] + fromhigh[...]
    for b in range(2):
        t = tot[:, 64 * b : 64 * b + 64]
        hi, lo = two_terms(weights_of(t[0:64], t[64:65]))
        tt[b] = jnp.concatenate([hi, hi, lo], axis=1)
    lane = lax.broadcasted_iota(jnp.int32, (64, 128), 1)

    @pl.loop(0, 4)
    def _(i):
        for half in range(2):
            n = 2 * i + half
            fetch(n).wait()
            upd = []
            for b in range(2):
                for rr in range(8):
                    hi, lo = two_terms(sv[n, b ^ odd, rr])
                    cols = pl.ds(128 * rr, 128)
                    rhs[half, b, 0:64, cols] = hi
                    rhs[half, b, 64:128, cols] = lo
                    rhs[half, b, 128:192, cols] = hi
                upd.append(
                    lax.dot_general(
                        tt[b], rhs[half, b], (((1,), (0,)), ((), ())), preferred_element_type=F32
                    )
                )
            m8 = [
                mean[b ^ odd, pl.ds(pl.multiple_of(kept_at(n), 8), 8), :] for b in range(2)
            ]
            sea8 = [sea[b, pl.ds(pl.multiple_of(8 * n, 8), 8), :] for b in range(2)]
            for rr in range(8):
                res = []
                for b in range(2):
                    x = sv[n, b ^ odd, rr]
                    up = upd[b][:, 128 * rr : 128 * rr + 128]
                    res.append((m8[b][rr : rr + 1] + x) + sea8[b][rr : rr + 1] * (up - x))
                at = pl.ds(YS * rr, 64)
                ys[half, 0, at, :] = jnp.where(lane < 64, res[0], pltpu.roll(res[1], 64, 1))
                ys[half, 1, at, :] = jnp.where(lane < 64, pltpu.roll(res[0], 64, 1), res[1])

            @pl.when(i > 0)
            def _(half=half, n=n):
                store(half, n).wait()

            for m in range(64):
                for lev in range(2):
                    ov[half, m, lev] = ys[half, lev, pl.ds(m, 8, stride=YS), :]
            store(half, n).start()

    for half in range(2):
        store(half, jnp.int32(6 + half)).wait()


def analysis(own, fromlow, fromhigh, s, mean, sea):
    return pl.pallas_call(
        analysis_kernel,
        out_shape=jax.ShapeDtypeStruct((64, 2, 64, 128), F32),
        in_specs=[VM] * 5 + [ANY],
        out_specs=ANY,
        scratch_shapes=[
            pltpu.VMEM((8, 2, 8, 64, 128), F32),
            pltpu.VMEM((2, 64, 192), BF16),
            pltpu.VMEM((2, 2, 192, 1024), BF16),
            pltpu.VMEM((2, 2, 8 * YS, 128), F32),
            pltpu.VMEM((2, 64, 2, 8, 128), F32),
            pltpu.SemaphoreType.DMA((8,)),
            pltpu.SemaphoreType.DMA((2,)),
        ],
        compiler_params=params(),
        cost_estimate=us(8),
        name="analysis",
    )(near(own), near(fromlow), near(fromhigh), mean, sea, s)


def per_device(state, diffusivity, land_sea, obs_value, obs_var, obs_cell, obs_count):
    tiles = lax.axis_size("tile")
    up = [(i, i + 1) for i in range(tiles - 1)]
    down = [(i + 1, i) for i in range(tiles - 1)]
    swap = lambda k: [(i, i ^ k) for i in range(4)]

    mem = lambda v, k: lax.ppermute(v, "mem", swap(k))
    after = lax.optimization_barrier

    a = list(forecast_first(state, diffusivity, land_sea))
    a2, a3, a1 = mem(a[2], 2), mem(a[3], 3), mem(a[1], 1)
    hup, hdn, a1 = after((a[4], a[5], a1))
    above = lax.ppermute(hup, "tile", up)
    below = lax.ppermute(hdn, "tile", down)
    a[0], land_b = after((a[0], land_sea))
    b = list(forecast_inner(state, diffusivity, land_b))
    b2, b3, b1 = mem(b[2], 2), mem(b[3], 3), mem(b[1], 1)
    land_e, b[0] = after((land_sea, b[0]))
    e = list(forecast_edge(state, diffusivity, land_e, near(above), near(below)))
    e2, e3, e1 = mem(e[2], 2), mem(e[3], 3), mem(e[1], 1)
    obs_cell, e1 = after((obs_cell, e1))
    wu, sea = cell_weights(obs_count, obs_cell, obs_value, obs_var, land_sea)
    held = gram_call("first", (0, 1), 2, 1, (24, 32), (a[0], a1, a2, a3), wu, None, 0.1)
    held = gram_call("inner", (0, 1), 1, 0, (8, 16), (b[0], b1, b2, b3), wu, held, 0.1)
    edge = (e[0], e1, e2, e3)
    s, mean, border, acc = end_call(0, edge, wu, held, 3)
    border = lax.ppermute(border, "mem", [(1, 2), (2, 1)])
    s, mean, mid, core = end_call(1, edge, wu, (acc, s, mean), 4)
    core, border = after((core, border))
    core = mem(core, 1)
    to_low, own, to_high = join(mid, core, border)
    fromlow = lax.ppermute(to_high, "tile", up)
    fromhigh = lax.ppermute(to_low, "tile", down)
    return analysis(own, fromlow, fromhigh, s, mean, sea)


def solution(mesh):
    return jax.shard_map(
        per_device,
        mesh=mesh,
        in_specs=(
            P("mem", None, "tile", None),
            P("tile", None),
            P("tile", None),
            P("tile", "mem", None),
            P("tile", "mem", None),
            P("tile", "mem", None),
            P("tile", "mem"),
        ),
        out_specs=P(None, None, "tile", "mem"),
        check_vma=False,
    )
```

```python
import functools

import jax
import jax.numpy as jnp
from jax import lax
from jax.experimental import pallas as pl
from jax.experimental.pallas import tpu as pltpu
from jax.sharding import PartitionSpec as P

NSI = 4
LOC = 48.0
BS = 64
UNROLL = 4
UNROLL_B = 6
ML = 16
NE = 16
F32 = jnp.float32
BF16 = jnp.bfloat16
VMEM_LIMIT = 56 * 1024 * 1024
HIGHEST = lax.Precision.HIGHEST


def params(**kw):
    return pltpu.CompilerParams(vmem_limit_bytes=VMEM_LIMIT, **kw)


def two_terms(x):
    hi = x.astype(BF16)
    lo = (x - hi.astype(F32)).astype(BF16)
    return hi, lo


def pack_store(zs, z, row, lane):
    low = lane < 64
    for q in range(4):
        r0 = pltpu.roll(z[0][q], 64, 1)
        r1 = pltpu.roll(z[1][q], 64, 1)
        pair = (jnp.where(low, z[0][q], r1), jnp.where(low, r0, z[1][q]))
        for b in range(2):
            zs[q, b ^ (q & 1), row] = pair[b]


def fill_md(md, dif, land, rows):
    for r8 in sorted({r // 8 for r in rows}):
        m = land[8 * r8 : 8 * r8 + 8, :].astype(F32) * dif[8 * r8 : 8 * r8 + 8, :]
        for j in range(8):
            if 8 * r8 + j in rows:
                for q in range(4):
                    md[8 * r8 + j, q] = jnp.broadcast_to(
                        m[j : j + 1, 128 * q : 128 * q + 128], (8, 128)
                    )


def md_row(md, r):
    return [jnp.concatenate([md[r, q], md[r, q]], axis=0) for q in range(4)]


class Rows:
    def __init__(self, state, xs, sems, segments):
        self.n = sum(length for _, length in segments)
        self.stride = 2 * self.n + 8
        self.flat = xs.reshape(4 * ML * self.stride, 128)
        self.segments = segments
        self.copies = {}
        for lev in range(2):
            at = 0
            for i, (start, length) in enumerate(segments):
                self.copies[lev, i] = [
                    pltpu.make_async_copy(
                        state.at[:, lev, pl.ds(start, length), pl.ds(128 * q, 128)],
                        xs.at[q, :, pl.ds(lev * self.n + at, length)],
                        sems.at[lev, i * 4 + q],
                    )
                    for q in range(4)
                ]
                at += length

    def start(self, order=None):
        for i in order or range(len(self.segments)):
            for lev in range(2):
                for c in self.copies[lev, i]:
                    c.start()

    def wait(self, lev, which=None):
        for i in which or range(len(self.segments)):
            for c in self.copies[lev, i]:
                c.wait()

    def offset(self, r):
        at = 0
        for start, length in self.segments:
            if start <= r < start + length:
                return r - start + at
            at += length
        raise ValueError(r)

    def load(self, lev, off):
        return [
            self.flat[pl.ds(q * ML * self.stride + lev * self.n + off, ML, stride=self.stride), :]
            for q in range(4)
        ]


class Stencil:
    def __init__(self, x, y):
        self.x = x
        self.y = y
        self.lane = lax.broadcasted_iota(jnp.int32, (ML, 128), 1)

    def put(self, ref, p, lev, tiles):
        for q in range(4):
            ref[p, lev, :, pl.ds(128 * q, 128)] = tiles[q]

    def step(self, ref, p, lev, md):
        mid = [ref[p, lev, :, pl.ds(128 * q, 128)] for q in range(4)]
        fwd = [pltpu.roll(t, 1, 1) for t in mid]
        bwd = [pltpu.roll(t, 127, 1) for t in mid]
        zero = jnp.zeros_like(mid[0])
        out = []
        for q in range(4):
            cols = pl.ds(128 * q, 128)
            left = jnp.where(self.lane == 0, fwd[q - 1] if q > 0 else zero, fwd[q])
            right = jnp.where(self.lane == 127, bwd[q + 1] if q < 3 else zero, bwd[q])
            near = (ref[p - 1, lev, :, cols] + ref[p + 1, lev, :, cols]) + (left + right)
            out.append(mid[q] + md[q] * (near - 4.0 * mid[q]))
        return out


class Sender:
    def __init__(self, zs, outs, me, sems):
        self.zs = zs
        self.outs = outs
        self.me = me
        self.sems = sems
        self.copies = []

    def send(self, at, length):
        for k in range(4):
            c = pltpu.make_async_copy(
                self.zs.at[self.me ^ k, :, pl.ds(at, length)],
                self.outs[k].at[:, pl.ds(at, length)],
                self.sems.at[len(self.copies)],
            )
            c.start()
            self.copies.append(c)

    def wait(self):
        for c in self.copies:
            c.wait()


SEG_A = ((16, 24), (40, 24), (0, 8))
SEG_B = ((0, 32),)
SEG_C = ((0, 16), (48, 16))
ROWS_A = (24, 32)
ROWS_B = (8, 16)


def plain_rows(rows, st, md, zs, sender, r0, n, parts):
    off = rows.offset(r0 - 2)
    lane = lax.broadcasted_iota(jnp.int32, (ML, 128), 1)
    low, made = 0, 1
    for segment, high in parts:
        for lev in range(2):
            rows.wait(lev, (segment,))

            @pl.loop(low, high, unroll=2)
            def _(p, lev=lev):
                st.put(st.x, p, lev, rows.load(lev, off + p))

        @pl.loop(made, high - 1, unroll=UNROLL_B)
        def _(p):
            m = md_row(md, p + (r0 - 2))
            for lev in range(2):
                st.put(st.y, p, lev, st.step(st.x, p, lev, m))

        low, made = high, high - 1

    for blk in range(n // 8):

        @pl.loop(8 * blk, 8 * blk + 8, unroll=UNROLL)
        def _(i):
            m = md_row(md, i + r0)
            pack_store(zs, [st.step(st.y, i + 2, lev, m) for lev in range(2)], i, lane)

        sender.send(8 * blk, 8)
    sender.wait()


def first_rows_kernel(
    state, dif, land, o0, o1, o2, o3, hup, hdn, xs, zs, md, x, y, isem, osem
):
    rows = Rows(state, xs, isem, SEG_A)
    rows.start()
    r0, n = ROWS_A
    fill_md(md, dif, land, [0, 63, *range(r0 - 1, r0 + n + 1)])
    st = Stencil(x, y)
    sender = Sender(zs, (o0, o1, o2, o3), lax.axis_index("mem"), osem)
    plain_rows(rows, st, md, zs, sender, r0, n, ((0, 18), (1, 36)))
    for lev in range(2):
        rows.wait(lev, (2,))
    for j in range(2):
        for lev in range(2):
            for ref, r in ((hdn, j), (hup, 62 + j)):
                v = rows.load(lev, rows.offset(r))
                for q in range(4):
                    ref[pl.ds(j * 32 + lev * 16, 16), pl.ds(128 * q, 128)] = v[q]
    for ref, r in ((hup, 63), (hdn, 0)):
        for q in range(4):
            ref[64:72, 128 * q : 128 * q + 128] = md[r, q]


def inner_rows_kernel(
    state, dif, land, o0, o1, o2, o3, xs, zs, md, x, y, isem, osem
):
    rows = Rows(state, xs, isem, SEG_B)
    rows.start()
    r0, n = ROWS_B
    fill_md(md, dif, land, range(r0 - 1, r0 + n + 1))
    st = Stencil(x, y)
    sender = Sender(zs, (o0, o1, o2, o3), lax.axis_index("mem"), osem)
    plain_rows(rows, st, md, zs, sender, r0, n, ((0, n + 4),))


def edge_rows_kernel(
    state, dif, land, above, below, o0, o1, o2, o3, xs, zs, md, x, y, isem, osem
):
    rows = Rows(state, xs, isem, SEG_C)
    rows.start()
    fill_md(md, dif, land, [*range(9), *range(55, 64)])
    st = Stencil(x, y)
    sender = Sender(zs, (o0, o1, o2, o3), lax.axis_index("mem"), osem)
    lane = lax.broadcasted_iota(jnp.int32, (ML, 128), 1)
    for ref, p0 in ((above, 0), (below, 22)):
        for j in range(2):
            for lev in range(2):
                at = pl.ds(j * 32 + lev * 16, 16)
                st.put(x, p0 + j, lev, [ref[at, 128 * q : 128 * q + 128] for q in range(4)])
    for lev in range(2):
        rows.wait(lev)

        @pl.loop(0, 10, unroll=2)
        def _(i, lev=lev):
            st.put(x, i + 2, lev, rows.load(lev, i))
            st.put(x, i + 12, lev, rows.load(lev, i + 22))

    def outside(ref):
        tiles = [ref[64:72, 128 * q : 128 * q + 128] for q in range(4)]
        return [jnp.concatenate([t, t], axis=0) for t in tiles]

    for p, ref in ((1, above), (22, below)):
        for lev in range(2):
            st.put(y, p, lev, st.step(x, p, lev, outside(ref)))

    @pl.loop(0, 9, unroll=3)
    def _(i):
        m = md_row(md, i)
        w = md_row(md, i + 55)
        for lev in range(2):
            st.put(y, i + 2, lev, st.step(x, i + 2, lev, m))
            st.put(y, i + 13, lev, st.step(x, i + 13, lev, w))

    for blk in range(2):

        @pl.loop(0, 8, unroll=UNROLL)
        def _(i, blk=blk):
            m = md_row(md, i + 56 * blk)
            z = [st.step(y, i + 2 + 12 * blk, lev, m) for lev in range(2)]
            pack_store(zs, z, i + 8 * blk, lane)

        sender.send(8 * blk, 8)
    sender.wait()


ANY = pl.BlockSpec(memory_space=pl.ANY)
VM = pl.BlockSpec(memory_space=pltpu.VMEM)


def us(t):
    return pl.CostEstimate(
        flops=int(t * 1.1e9), bytes_accessed=int(t * 3.4e6), transcendentals=0
    )


def piece(n):
    return jax.ShapeDtypeStruct((2, n, ML, 128), F32)


def forecast_call(kernel, name, segments, n, count, outs, extra_out, args, cost):
    loaded = sum(length for _, length in segments)
    kept = (count, 2, ML, 512)
    return pl.pallas_call(
        kernel,
        out_shape=outs + extra_out,
        in_specs=[ANY] + [VM] * (len(args) - 1),
        out_specs=[ANY] * len(outs) + [VM] * len(extra_out),
        scratch_shapes=[
            pltpu.VMEM((4, ML, 2 * loaded + 8, 128), F32),
            pltpu.VMEM((4, 2, n, ML, 128), F32),
            pltpu.VMEM((64, 4, 8, 128), F32),
            pltpu.VMEM(kept, F32),
            pltpu.VMEM(kept, F32),
            pltpu.SemaphoreType.DMA((2, 4 * len(segments))),
            pltpu.SemaphoreType.DMA((n // 8 * len(outs),)),
        ],
        compiler_params=params(),
        cost_estimate=us(cost),
        name=name,
    )(*args)


def forecast_first(*args):
    n = ROWS_A[1]
    halo = pltpu.VMEM((72, 512), F32)
    return forecast_call(
        first_rows_kernel, "forecast_first", SEG_A, n, n + 4, [piece(n)] * 4, [halo, halo], args, 5
    )


def forecast_inner(*args):
    n = ROWS_B[1]
    return forecast_call(
        inner_rows_kernel, "forecast_inner", SEG_B, n, n + 4, [piece(n)] * 4, [], args, 9
    )


def forecast_edge(*args):
    return forecast_call(
        edge_rows_kernel,
        "forecast_edge",
        SEG_C,
        NE,
        24,
        [piece(NE)] * 4,
        [],
        args,
        0.1,
    )


def dot_nt(a, b):
    return lax.dot_general(a, b, (((1,), (1,)), ((), ())), preferred_element_type=F32)


def weight_kernel(count, cell, value, var, land, out, sea_out):
    me = lax.axis_index("mem")
    odd = me & 1
    slots = cell.shape[2]
    rows64 = lax.broadcasted_iota(jnp.int32, (64, slots), 0)
    rows128 = lax.broadcasted_iota(jnp.int32, (128, slots), 0)
    slot = lax.broadcasted_iota(jnp.int32, (1, slots), 1)
    sea = land[:, pl.ds(pl.multiple_of(me * 128, 128), 128)].astype(F32)
    lane = lax.broadcasted_iota(jnp.int32, (64, 128), 1)
    turned = pltpu.roll(sea, 64, 1)
    seas = (jnp.where(lane < 64, sea, turned), jnp.where(lane < 64, turned, sea))
    for b in range(2):
        c = cell[0, b : b + 1, :]
        live = slot < count[0, b]
        w = jnp.where(live, 1.0 / var[0, b : b + 1, :], 0.0)
        u = w * value[0, b : b + 1, :]
        at_row = rows64 == ((c >> 6) & 63)
        at_lane = rows128 == (((c >> 12) << 6) | (c & 63))
        terms = []
        for v in (w, u):
            hi = v.astype(BF16).astype(F32)
            terms += [jnp.where(at_row, t, 0.0).astype(BF16) for t in (hi, v - hi)]
        lhs = jnp.concatenate(terms, axis=0)
        rhs = jnp.where(at_lane, 1.0, 0.0).astype(BF16)
        full = dot_nt(lhs, rhs)
        fs = b ^ odd
        for n in range(2):
            v = (full[128 * n : 128 * n + 64] + full[128 * n + 64 : 128 * n + 128]) * seas[b]
            out[fs, n, 0:48] = v[8:56]
            out[fs, n, 48:56] = v[0:8]
            out[fs, n, 56:64] = v[56:64]
        sea_out[b] = seas[b]


def cell_weights(count, cell, value, var, land):
    return pl.pallas_call(
        weight_kernel,
        out_shape=[
            jax.ShapeDtypeStruct((2, 2, 64, 128), F32),
            jax.ShapeDtypeStruct((2, 64, 128), F32),
        ],
        in_specs=[pl.BlockSpec(memory_space=pltpu.SMEM), VM, VM, VM, VM],
        out_specs=[VM, VM],
        compiler_params=params(),
        cost_estimate=us(0.1),
        name="cell_weights",
    )(count, cell, value, var, land)


def gauss(off):
    return jnp.exp(-(off * off) / (2.0 * LOC * LOC))


GR = 208


def gram_rows(pieces, s_out, mean_out, wu, rows, acc, fs, lh, rh, rl, xo, me, begin=None):
    for k in range(4):
        at = pl.multiple_of((me ^ k) * ML, ML)
        xo[:, pl.ds(at, ML), :] = pieces[k][0]
    sub = lax.broadcasted_iota(jnp.int32, (8, 128), 0)
    c = (lax.broadcasted_iota(jnp.int32, (1, 128), 1) & 63).astype(F32)
    ec = [gauss(c - 31.5 - 64.0 * j) for j in (-1, 0, 1)]
    sub16 = lax.broadcasted_iota(jnp.int32, (16, 128), 0)
    for half in range(len(rows)):
        r = (sub + rows[half]).astype(F32)
        er = [gauss(r - 31.5 - 64.0 * i) for i in (-1, 0, 1)]
        w = wu[0, 0, 8 * half : 8 * half + 8, :]
        u = wu[0, 1, 8 * half : 8 * half + 8, :]
        wi = [w * e for e in er]
        ui = [u * e for e in er]
        for j8 in range(8):
            rr = 8 * half + j8
            x = xo[rr]
            mean = jnp.sum(x, axis=0, keepdims=True) * (1.0 / 64.0)
            mean_out[0, rr : rr + 1, :] = mean
            s = x - mean
            s_out[0, rr] = s
            cols = pl.ds(128 * rr, 128)
            drives = jnp.zeros((16, 128), F32)
            for i in range(3):
                wrow = wi[i][j8 : j8 + 1]
                hi, lo = two_terms(s * wrow)
                lh[pl.ds(64 * i, 64), cols] = hi
                lh[pl.ds(GR + 64 * i, 64), cols] = lo
                drives = jnp.where(sub16 == i, ui[i][j8 : j8 + 1] - wrow * mean, drives)
            hi, lo = two_terms(drives)
            lh[pl.ds(192, 16), cols] = hi
            lh[pl.ds(GR + 192, 16), cols] = lo
            for j in range(3):
                hi, lo = two_terms(s * ec[j])
                rh[pl.ds(64 * j, 64), cols] = hi
                rl[pl.ds(64 * j, 64), cols] = lo
    if begin is not None:
        begin()
    both = dot_nt(lh[...], rh[...])
    acc[fs] += both[0:GR] + both[GR : 2 * GR] + dot_nt(lh[0:GR, :], rl[...])


def gram_kernel(halves, groups, rows, stage, *refs):
    me = lax.axis_index("mem")
    g = pl.program_id(0)
    refs = list(refs)
    pieces = [refs.pop(0) for _ in range(4)]
    wu = refs.pop(0)
    acc_in = None
    if stage != "first":
        acc_in = refs.pop(0)
        del refs[0:2]
    acc, s_out, mean_out = (refs.pop(0) for _ in range(3))
    tmp = refs

    @pl.when(g == 0)
    def _():
        acc[...] = jnp.zeros_like(acc) if acc_in is None else acc_in[...]

    if len(halves) == 2:
        fs = g // groups
    else:
        fs = halves[0]
    first = [r + 16 * (g % groups) for r in rows]
    gram_rows(pieces, s_out, mean_out, wu, first, acc, fs, *tmp, me)


def near(x):
    return pltpu.with_memory_space_constraint(x, pltpu.VMEM)


def end_kernel(fs, *refs):
    me = lax.axis_index("mem")
    odd = (me & 1) == 1
    refs = list(refs)
    pieces = [refs.pop(0).at[pl.ds(fs, 1)] for _ in range(4)]
    wu = refs.pop(0).at[pl.ds(fs, 1), :, pl.ds(48, 16)]
    acc_in = refs.pop(0)
    del refs[0:2]
    spread, mean = refs.pop(0), refs.pop(0)
    extra = [refs.pop(0) for _ in range(2)]
    acc = refs.pop(0) if fs == 1 else extra[1]
    s_out, mean_out, sems = (refs.pop(0) for _ in range(3))
    acc[...] = acc_in[...]
    copies = [
        pltpu.make_async_copy(
            s_out, spread.at[pl.ds(fs, 1), pl.ds(48, 16)], sems.at[0]
        ),
        pltpu.make_async_copy(
            mean_out, mean.at[pl.ds(fs, 1), pl.ds(48, 16)], sems.at[1]
        ),
    ]

    def begin():
        for c in copies:
            c.start()

    gram_rows(pieces, s_out, mean_out, wu, (0, 56), acc, fs, *refs, me, begin)
    if fs == 0:
        d = acc[0]
        extra[0][...] = jnp.where(odd, d[:, 128:192], d[:, 0:64])
    else:
        b0 = acc[me & 1]
        b1 = acc[1 - (me & 1)]
        extra[0][...] = jnp.concatenate(
            [b0[:, 64:128] + b1[:, 0:64], b0[:, 128:192] + b1[:, 64:128]], axis=1
        )
        extra[1][...] = jnp.where(odd, b0[:, 0:64], b1[:, 128:192])
    for c in copies:
        c.wait()


def end_call(fs, pieces, wu, held, cost):
    acc, spread, mean = held
    if fs == 0:
        extra = [pltpu.VMEM((GR, 64), F32), pltpu.VMEM(acc.shape, F32)]
    else:
        extra = [pltpu.VMEM((GR, 128), F32), pltpu.VMEM((GR, 64), F32)]
    args = [near(p) for p in pieces] + [near(wu), near(acc), spread, mean]
    return pl.pallas_call(
        functools.partial(end_kernel, fs),
        out_shape=[
            jax.ShapeDtypeStruct(spread.shape, F32),
            jax.ShapeDtypeStruct(mean.shape, F32),
        ]
        + extra,
        in_specs=[VM] * 6 + [ANY] * 2,
        out_specs=[ANY, ANY, VM, VM],
        input_output_aliases={6: 0, 7: 1},
        scratch_shapes=[pltpu.VMEM(acc.shape, F32)] * fs
        + [
            pltpu.VMEM((1, 16, 64, 128), F32),
            pltpu.VMEM((1, 16, 128), F32),
            pltpu.SemaphoreType.DMA((2,)),
            pltpu.VMEM((2 * GR, 2048), BF16),
            pltpu.VMEM((192, 2048), BF16),
            pltpu.VMEM((192, 2048), BF16),
            pltpu.VMEM((16, 64, 128), F32),
        ],
        compiler_params=params(),
        cost_estimate=us(cost),
        name=("gram_border", "gram_last")[fs],
    )(*args)


def WHOLE(shape):
    return pl.BlockSpec(shape, lambda g: (0,) * len(shape))


def gram_call(stage, halves, groups, kept, rows, pieces, wu, held, cost):
    n = 16
    fs_of = (lambda g: g // groups) if len(halves) == 2 else (lambda g: halves[0])
    sub = lambda g: g % groups
    ins = [pl.BlockSpec((1, n, ML, 128), lambda g: (fs_of(g), sub(g), 0, 0))] * 4
    ins.append(pl.BlockSpec((1, 2, n, 128), lambda g: (fs_of(g), 0, kept + sub(g), 0)))
    args = list(pieces) + [wu]
    acc_shape = (2, GR, 192)
    outs = [
        pltpu.VMEM(acc_shape, F32),
        jax.ShapeDtypeStruct((2, BS, 64, 128), F32),
        jax.ShapeDtypeStruct((2, BS, 128), F32),
    ]
    out_specs = [
        WHOLE(acc_shape),
        pl.BlockSpec((1, n, 64, 128), lambda g: (fs_of(g), kept + sub(g), 0, 0)),
        pl.BlockSpec((1, n, 128), lambda g: (fs_of(g), kept + sub(g), 0)),
    ]
    aliases = {}
    if stage != "first":
        aliases = {len(args) + 1: 1, len(args) + 2: 2}
        ins += [WHOLE(acc_shape)] + [pl.BlockSpec(memory_space=pl.ANY)] * 2
        args += list(held)
    return pl.pallas_call(
        functools.partial(gram_kernel, halves, groups, rows, stage),
        grid=(len(halves) * groups,),
        out_shape=outs,
        in_specs=ins,
        out_specs=out_specs,
        input_output_aliases=aliases,
        scratch_shapes=[
            pltpu.VMEM((2 * GR, 128 * n), BF16),
            pltpu.VMEM((192, 128 * n), BF16),
            pltpu.VMEM((192, 128 * n), BF16),
            pltpu.VMEM((n, 64, 128), F32),
        ],
        compiler_params=params(),
        cost_estimate=us(cost),
        name="gram_" + stage,
    )(*args)


def join_kernel(mid, core, border, down, own, up):
    odd = (lax.axis_index("mem") & 1) == 1
    c = core[...]
    b = border[...]
    q = mid[...] + jnp.concatenate([jnp.where(odd, c, b), jnp.where(odd, b, c)], axis=1)
    for i, ref in enumerate((down, own, up)):
        ref[0:64] = q[64 * i : 64 * i + 64]
        ref[64:72] = jnp.broadcast_to(q[192 + i : 193 + i], (8, 128))


def join(mid, core, border):
    one = pltpu.VMEM((72, 128), F32)
    mid, core, border = near(mid), near(core), near(border)
    return pl.pallas_call(
        join_kernel,
        out_shape=[one, one, one],
        in_specs=[VM, VM, VM],
        out_specs=[VM, VM, VM],
        compiler_params=params(),
        cost_estimate=us(0.1),
        name="join_grams",
    )(mid, core, border)


def dot32(a, b):
    return lax.dot_general(
        a, b, (((1,), (0,)), ((), ())), precision=HIGHEST, preferred_element_type=F32
    )


def weights_of(gram, drive):
    n = gram.shape[0]
    eye = (
        lax.broadcasted_iota(jnp.int32, (n, n), 0) == lax.broadcasted_iota(jnp.int32, (n, n), 1)
    ).astype(F32)
    system = (n - 1.0) * eye + gram
    squares = jnp.sum(jnp.sum(system * system, axis=1, keepdims=True), axis=0, keepdims=True)
    frob = jnp.sqrt(squares)
    iterate = system / frob
    root = None
    for it in range(NSI):
        prod = iterate if root is None else dot32(root, iterate)
        corr = 1.5 * eye - 0.5 * prod
        if it < NSI - 1:
            iterate = dot32(iterate, corr)
        root = corr if root is None else dot32(corr, root)
    half = root / jnp.sqrt(frob)
    row = dot32(dot32(jnp.broadcast_to(drive, (8, n)), half), half)
    return jnp.sqrt(n - 1.0) * half + row[0:1]


YS = 68


def kept_at(n):
    return jnp.where(n == 0, 6, jnp.where(n == 7, 7, n - 1)) * 8


def analysis_kernel(
    own, fromlow, fromhigh, mean, sea, spread, out, sv, tt, rhs, ys, ov, isem, osem
):
    me = lax.axis_index("mem")
    odd = me & 1

    def fetch(n):
        rows = pl.ds(pl.multiple_of(kept_at(n), 8), 8)
        return pltpu.make_async_copy(spread.at[:, rows], sv.at[n], isem.at[n])

    def store(half, n):
        rows = pl.ds(pl.multiple_of(8 * n, 8), 8)
        return pltpu.make_async_copy(ov.at[half], out.at[:, :, rows], osem.at[half])

    for n in range(8):
        fetch(jnp.int32(n)).start()
    tot = own[...] + fromlow[...] + fromhigh[...]
    for b in range(2):
        t = tot[:, 64 * b : 64 * b + 64]
        hi, lo = two_terms(weights_of(t[0:64], t[64:65]))
        tt[b] = jnp.concatenate([hi, hi, lo], axis=1)
    lane = lax.broadcasted_iota(jnp.int32, (64, 128), 1)

    @pl.loop(0, 4)
    def _(i):
        for half in range(2):
            n = 2 * i + half
            fetch(n).wait()
            upd = []
            for b in range(2):
                for rr in range(8):
                    hi, lo = two_terms(sv[n, b ^ odd, rr])
                    cols = pl.ds(128 * rr, 128)
                    rhs[half, b, 0:64, cols] = hi
                    rhs[half, b, 64:128, cols] = lo
                    rhs[half, b, 128:192, cols] = hi
                upd.append(
                    lax.dot_general(
                        tt[b], rhs[half, b], (((1,), (0,)), ((), ())), preferred_element_type=F32
                    )
                )
            m8 = [
                mean[b ^ odd, pl.ds(pl.multiple_of(kept_at(n), 8), 8), :] for b in range(2)
            ]
            sea8 = [sea[b, pl.ds(pl.multiple_of(8 * n, 8), 8), :] for b in range(2)]
            for rr in range(8):
                res = []
                for b in range(2):
                    x = sv[n, b ^ odd, rr]
                    up = upd[b][:, 128 * rr : 128 * rr + 128]
                    res.append((m8[b][rr : rr + 1] + x) + sea8[b][rr : rr + 1] * (up - x))
                at = pl.ds(YS * rr, 64)
                ys[half, 0, at, :] = jnp.where(lane < 64, res[0], pltpu.roll(res[1], 64, 1))
                ys[half, 1, at, :] = jnp.where(lane < 64, pltpu.roll(res[0], 64, 1), res[1])

            @pl.when(i > 0)
            def _(half=half, n=n):
                store(half, n).wait()

            for m in range(64):
                for lev in range(2):
                    ov[half, m, lev] = ys[half, lev, pl.ds(m, 8, stride=YS), :]
            store(half, n).start()

    for half in range(2):
        store(half, jnp.int32(6 + half)).wait()


def analysis(own, fromlow, fromhigh, s, mean, sea):
    return pl.pallas_call(
        analysis_kernel,
        out_shape=jax.ShapeDtypeStruct((64, 2, 64, 128), F32),
        in_specs=[VM] * 5 + [ANY],
        out_specs=ANY,
        scratch_shapes=[
            pltpu.VMEM((8, 2, 8, 64, 128), F32),
            pltpu.VMEM((2, 64, 192), BF16),
            pltpu.VMEM((2, 2, 192, 1024), BF16),
            pltpu.VMEM((2, 2, 8 * YS, 128), F32),
            pltpu.VMEM((2, 64, 2, 8, 128), F32),
            pltpu.SemaphoreType.DMA((8,)),
            pltpu.SemaphoreType.DMA((2,)),
        ],
        compiler_params=params(),
        cost_estimate=us(8),
        name="analysis",
    )(near(own), near(fromlow), near(fromhigh), near(mean), near(sea), s)


def per_device(state, diffusivity, land_sea, obs_value, obs_var, obs_cell, obs_count):
    tiles = lax.axis_size("tile")
    up = [(i, i + 1) for i in range(tiles - 1)]
    down = [(i + 1, i) for i in range(tiles - 1)]
    swap = lambda k: [(i, i ^ k) for i in range(4)]

    mem = lambda v, k: lax.ppermute(v, "mem", swap(k))
    after = lax.optimization_barrier

    a = list(forecast_first(state, diffusivity, land_sea))
    a2, a3, a1 = mem(a[2], 2), mem(a[3], 3), mem(a[1], 1)
    hup, hdn, a1 = after((a[4], a[5], a1))
    above = lax.ppermute(hup, "tile", up)
    below = lax.ppermute(hdn, "tile", down)
    a[0], land_b = after((a[0], land_sea))
    b = list(forecast_inner(state, diffusivity, land_b))
    b2, b3, b1 = mem(b[2], 2), mem(b[3], 3), mem(b[1], 1)
    land_e, b[0] = after((land_sea, b[0]))
    e = list(forecast_edge(state, diffusivity, land_e, near(above), near(below)))
    e2, e3, e1 = mem(e[2], 2), mem(e[3], 3), mem(e[1], 1)
    obs_cell, e1 = after((obs_cell, e1))
    wu, sea = cell_weights(obs_count, obs_cell, obs_value, obs_var, land_sea)
    held = gram_call("first", (0, 1), 2, 1, (24, 32), (a[0], a1, a2, a3), wu, None, 0.1)
    held = gram_call("inner", (0, 1), 1, 0, (8, 16), (b[0], b1, b2, b3), wu, held, 0.1)
    edge = (e[0], e1, e2, e3)
    s, mean, border, acc = end_call(0, edge, wu, held, 3)
    border = lax.ppermute(border, "mem", [(1, 2), (2, 1)])
    s, mean, mid, core = end_call(1, edge, wu, (acc, s, mean), 4)
    core, border = after((core, border))
    core = mem(core, 1)
    to_low, own, to_high = join(mid, core, border)
    fromlow = lax.ppermute(to_high, "tile", up)
    fromhigh = lax.ppermute(to_low, "tile", down)
    return analysis(own, fromlow, fromhigh, s, mean, sea)


def solution(mesh):
    return jax.shard_map(
        per_device,
        mesh=mesh,
        in_specs=(
            P("mem", None, "tile", None),
            P("tile", None),
            P("tile", None),
            P("tile", "mem", None),
            P("tile", "mem", None),
            P("tile", "mem", None),
            P("tile", "mem"),
        ),
        out_specs=P(None, None, "tile", "mem"),
        check_vma=False,
    )
```
